512 devices in a mesh: seq: 64 (over y, z_hi, core), head: 8 (over x, z_lo).
Axes of the slice: x: 4, y: 8, z: 8 (z_hi: 4, z_lo: 2; z = z_hi * 2 + z_lo), core: 2. Of those that a mesh axis runs over, the one named last changes fastest.
Arguments:
- queries: bfloat16 [8192, 8192], P(('seq', 'head')), may hold values from -6 to 6, as said below
- response_keys: bfloat16 [8192, 1024], P(('seq', 'head')), may hold values from -6 to 6
- response_values: bfloat16 [8192, 1024], P(('seq', 'head')), may hold values from -96 to 96
- shared_prompt_keys: bfloat16 [512, 1024], P('seq', 'head'), may hold values from -6 to 6
- shared_prompt_values: bfloat16 [512, 1024], P('seq', 'head'), may hold values from -96 to 96
- output_gradient: bfloat16 [8192, 8192], P(('seq', 'head')), may hold values from -24 to 24
- lengths: int32 [8], replicated, may hold values from 1 to 1024, 5120 in all
Outputs:
- attended: bfloat16 [8192, 8192], P('seq', 'head')
- query_grad: bfloat16 [8192, 8192], P('seq', 'head')
- response_key_gradient: bfloat16 [8192, 1024], P('seq', 'head')
- response_value_gradient: bfloat16 [8192, 1024], P('seq', 'head')
- prompt_key_gradient: float32 [512, 1024], P('seq', 'head')
- prompt_value_gradient: float32 [512, 1024], P('seq', 'head')
The draws below stay inside these ranges and needn't reach their ends.
Inputs may be any that keep to these rules, and one draw needn't show every extreme that they name: At the first position of each response, in the hidden draw, some queries may be large multiples of a fixed sign pattern. `lengths`: the longest response has exactly 1024 tokens.
All inputs are finite; a program needn't handle non-finite values.
Results may differ from the reference program's by a relative error of at most 0.03.
Values may be sent and summed in bfloat16 or wider, within the bound.
A program may use at most 64 MiB of HBM per device.

```python
import math
from functools import partial
import jax
import jax.numpy as jnp
import numpy as np
from jax import lax

QUERY_HEADS = 64
KEY_VALUE_HEADS = 8
HEAD_WIDTH = 128
RESPONSE_LENGTH = 1024
PROMPT_TOKENS = 512
RESPONSE_TOKENS = 8192
RESPONSE_COUNT = 8


def draw_queries(key, part):
    key = jax.random.fold_in(key, 7)
    value_rows = jnp.clip(jax.random.normal(key, (RESPONSE_TOKENS, QUERY_HEADS * HEAD_WIDTH), jnp.float32), -6.0, 6.0)
    return value_rows.astype(jnp.bfloat16)


def draw_shared_prompt_keys(key, part):
    key = jax.random.fold_in(key, 13)
    value_rows = jnp.clip(jax.random.normal(key, (PROMPT_TOKENS, KEY_VALUE_HEADS * HEAD_WIDTH), jnp.float32), -6.0, 6.0)
    return value_rows.astype(jnp.bfloat16)


def block_levels(key, shape, pieces, smallest, high):
    level = 1.0
    for dim, blocks in pieces:
        heights = jax.random.uniform(jax.random.fold_in(jax.random.fold_in(key, 6), dim), (blocks,), jnp.float32, smallest / len(pieces), high / len(pieces))
        level = level * jnp.repeat(jnp.exp(heights), shape[dim] // blocks).reshape((-1,) + (1,) * (len(shape) - 1 - dim))
    return level


def profile(number_of, total, reach, slope):
    portions = [(1 << 20) // math.isqrt(grade ** slope) + 1 for grade in range(2, number_of + 1)]
    surplus, holding = total - reach - (number_of - 1), [1] * (number_of - 1)
    while surplus > 0:
        candidates = [i for i in range(number_of - 1) if holding[i] < reach]
        pool, budget = sum([portions[i] for i in candidates]), surplus
        for i in candidates:
            more = min(reach - holding[i], max(1, budget * portions[i] // pool), surplus)
            holding[i] = holding[i] + more
            surplus = surplus - more
    return np.array([reach] + holding)


def ragged_sizes(rng, count, total, reach, lean):
    if count == 2:
        one = jax.random.randint(rng, (), max(1, total - reach), min(reach, total - 1) + 1)
        return jnp.stack([one, total - one])
    tallies = jnp.asarray(profile(count, total, reach, lean), jnp.int32)
    pairs = (count - 1) // 2
    donor, receiver = tallies[1:1 + 2 * pairs:2], tallies[2:2 + 2 * pairs:2]
    margin = jnp.minimum(donor - 1, reach - receiver)
    shifted = jax.random.randint(jax.random.fold_in(rng, 1), (pairs,), 0, 1 << 20) % (margin + 1)
    tallies = tallies.at[1:1 + 2 * pairs:2].set(donor - shifted).at[2:2 + 2 * pairs:2].set(receiver + shifted)
    return tallies[jax.random.permutation(jax.random.fold_in(rng, 2), count)]


def normal_values(key, extent, scale, reach, split=(), held_as=jnp.bfloat16):
    level = block_levels(key, extent, split, -0.22, 0.18) if split else 1.0
    array = jax.random.normal(key, extent, jnp.float32) * scale * level
    return jnp.minimum(jnp.maximum(array, -reach), reach).astype(held_as)


def setup_inputs(seed: int = 0) -> dict:
    keys = jax.random.split(jax.random.key(seed), 8)
    queries = draw_queries(jax.random.fold_in(keys[7], 71), 0)
    response_keys = normal_values(keys[1], (RESPONSE_TOKENS, KEY_VALUE_HEADS * HEAD_WIDTH), 1.0, 6.0, ((0, 512),))
    response_values = normal_values(keys[2], (RESPONSE_TOKENS, KEY_VALUE_HEADS * HEAD_WIDTH), 16.0, 96.0, ((0, 512),))
    shared_prompt_keys = draw_shared_prompt_keys(jax.random.fold_in(keys[7], 71), 0)
    shared_prompt_values = normal_values(keys[4], (PROMPT_TOKENS, KEY_VALUE_HEADS * HEAD_WIDTH), 16.0, 96.0, ((0, 64), (1, 8)))
    output_gradient = normal_values(keys[5], (RESPONSE_TOKENS, QUERY_HEADS * HEAD_WIDTH), 4.0, 24.0, ((0, 512),))
    lengths = ragged_sizes(keys[6], RESPONSE_COUNT, RESPONSE_COUNT * RESPONSE_LENGTH * 5 // 8, RESPONSE_LENGTH, 2).astype(jnp.int32)
    return dict(queries=queries, response_keys=response_keys, response_values=response_values, shared_prompt_keys=shared_prompt_keys, shared_prompt_values=shared_prompt_values, output_gradient=output_gradient, lengths=lengths)


def head_pass(head_item, key_mask, live_rows):
    head_queries, head_keys, head_values, head_grads = head_item
    score_scale = HEAD_WIDTH ** -0.5
    query_f32 = head_queries.astype(jnp.float32)
    key_f32 = head_keys.astype(jnp.float32)
    value_f32 = head_values.astype(jnp.float32)
    scores = jnp.einsum("tgd,cd->tgc", query_f32, key_f32) * score_scale
    scores = jnp.where(key_mask[:, None, :], scores, -jnp.inf)
    top_score = jnp.max(scores, axis=-1, keepdims=True)
    log_total = top_score + jnp.log(jnp.sum(jnp.exp(scores - top_score), axis=-1, keepdims=True))
    weights = jnp.exp(scores - log_total)
    weights_bf = weights.astype(jnp.bfloat16)
    outputs = jnp.einsum("tgc,cd->tgd", weights_bf.astype(jnp.float32), value_f32)
    attended = (outputs * live_rows.astype(jnp.float32)[:, None, None]).astype(jnp.bfloat16)
    masked = head_grads * live_rows.astype(jnp.bfloat16)[:, None, None]
    masked_f32 = masked.astype(jnp.float32)
    delta = jnp.sum(masked_f32 * attended.astype(jnp.float32), axis=-1)
    dweights = jnp.einsum("tgd,cd->tgc", masked_f32, value_f32)
    dscores = (weights * (dweights - delta[..., None])).astype(jnp.bfloat16)
    dscores_f32 = dscores.astype(jnp.float32)
    query_grad = (jnp.einsum("tgc,cd->tgd", dscores_f32, key_f32) * score_scale).astype(jnp.bfloat16)
    response_key_gradient = jnp.einsum("tgc,tgd->cd", dscores_f32, query_f32) * score_scale
    response_value_gradient = jnp.einsum("tgc,tgd->cd", weights_bf.astype(jnp.float32), masked_f32)
    return attended, query_grad, response_key_gradient, response_value_gradient


def reference(queries, response_keys, response_values, shared_prompt_keys, shared_prompt_values, output_gradient, lengths):
    group_count = QUERY_HEADS // KEY_VALUE_HEADS
    query_stack = queries.reshape(RESPONSE_COUNT, RESPONSE_LENGTH, KEY_VALUE_HEADS, group_count, HEAD_WIDTH).transpose(0, 2, 1, 3, 4)
    gradient_stack = output_gradient.reshape(RESPONSE_COUNT, RESPONSE_LENGTH, KEY_VALUE_HEADS, group_count, HEAD_WIDTH).transpose(0, 2, 1, 3, 4)
    key_stack = response_keys.reshape(RESPONSE_COUNT, RESPONSE_LENGTH, KEY_VALUE_HEADS, HEAD_WIDTH).transpose(0, 2, 1, 3)
    value_stack = response_values.reshape(RESPONSE_COUNT, RESPONSE_LENGTH, KEY_VALUE_HEADS, HEAD_WIDTH).transpose(0, 2, 1, 3)
    prompt_key_rows = shared_prompt_keys.reshape(PROMPT_TOKENS, KEY_VALUE_HEADS, HEAD_WIDTH).transpose(1, 0, 2)
    prompt_value_rows = shared_prompt_values.reshape(PROMPT_TOKENS, KEY_VALUE_HEADS, HEAD_WIDTH).transpose(1, 0, 2)
    positions = jnp.arange(RESPONSE_LENGTH)

    def per_response(running, response_item):
        resp_queries, resp_k, resp_v, resp_grads, length = response_item
        live_rows = positions < length
        own_mask = (positions[None, :] <= positions[:, None]) & (positions[None, :] < length)
        key_mask = jnp.concatenate([jnp.ones((RESPONSE_LENGTH, PROMPT_TOKENS), dtype=bool), own_mask], axis=1)
        joined_keys = jnp.concatenate([prompt_key_rows, resp_k], axis=1)
        joined_values = jnp.concatenate([prompt_value_rows, resp_v], axis=1)
        results = lax.map(partial(head_pass, key_mask=key_mask, live_rows=live_rows),
                          (resp_queries, joined_keys, joined_values, resp_grads))
        attended, query_grad, response_key_gradient, response_value_gradient = results
        running = (running[0] + response_key_gradient[:, :PROMPT_TOKENS], running[1] + response_value_gradient[:, :PROMPT_TOKENS])
        return running, (attended, query_grad, response_key_gradient[:, PROMPT_TOKENS:].astype(jnp.bfloat16),
                         response_value_gradient[:, PROMPT_TOKENS:].astype(jnp.bfloat16))

    starting_sums = (jnp.zeros((KEY_VALUE_HEADS, PROMPT_TOKENS, HEAD_WIDTH), jnp.float32), jnp.zeros((KEY_VALUE_HEADS, PROMPT_TOKENS, HEAD_WIDTH), jnp.float32))
    partial_sums, stacked = lax.scan(per_response, starting_sums, (query_stack, key_stack, value_stack, gradient_stack, lengths))
    attended, query_grad, response_key_gradient, response_value_gradient = stacked
    attended = attended.transpose(0, 2, 1, 3, 4).reshape(RESPONSE_TOKENS, QUERY_HEADS * HEAD_WIDTH)
    query_grad = query_grad.transpose(0, 2, 1, 3, 4).reshape(RESPONSE_TOKENS, QUERY_HEADS * HEAD_WIDTH)
    response_key_gradient = response_key_gradient.transpose(0, 2, 1, 3).reshape(RESPONSE_TOKENS, KEY_VALUE_HEADS * HEAD_WIDTH)
    response_value_gradient = response_value_gradient.transpose(0, 2, 1, 3).reshape(RESPONSE_TOKENS, KEY_VALUE_HEADS * HEAD_WIDTH)
    prompt_key_gradient = partial_sums[0].transpose(1, 0, 2).reshape(PROMPT_TOKENS, KEY_VALUE_HEADS * HEAD_WIDTH)
    prompt_value_gradient = partial_sums[1].transpose(1, 0, 2).reshape(PROMPT_TOKENS, KEY_VALUE_HEADS * HEAD_WIDTH)
    return attended, query_grad, response_key_gradient, response_value_gradient, prompt_key_gradient, prompt_value_gradient
```

```python
import functools
import math

import jax
import jax.numpy as jnp
from jax import lax
from jax.experimental import pallas as pl
from jax.experimental.pallas import tpu as pltpu
from jax.sharding import PartitionSpec as P

MESH = pl.DeviceIdType.MESH
BF = jnp.bfloat16
F32 = jnp.float32
W = 128
G = 8
KB = 256
CB = 256
NEG = -1e30


def dot_nt(a, b):
    return lax.dot_general(a, b, (((1,), (1,)), ((), ())), preferred_element_type=F32)


def dot_nn(a, b):
    return lax.dot_general(a, b, (((1,), (0,)), ((), ())), preferred_element_type=F32)


def kernel(
    dims,
    q_hbm,
    k_hbm,
    v_hbm,
    pk_ref,
    pv_ref,
    do_hbm,
    len_ref,
    att_ref,
    dq_ref,
    dkv_ref,
    prom_ref,
    q_all,
    do_all,
    kvb,
    kvt,
    pg,
    qr,
    dor,
    dot_t,
    s_scr,
    p_scr,
    mx,
    lx,
    o_acc,
    dq_acc,
    acc,
    prom_s,
    prom_r,
    prom_y,
    prom_z,
    xs,
    xr,
    zs,
    zr,
    a2a_send,
    a2a_recv,
    own_sem,
    pz_send,
    pz_recv,
    py_send,
    py_recv,
    pc_send,
    pc_recv,
    kz_send,
    kz_recv,
    kc_send,
    kc_recv,
    gx_send,
    gx_recv,
    gz_send,
    gz_recv,
    rc_send,
    rc_recv,
    ry_send,
    ry_recv,
    rz_send,
    rz_recv,
):
    H, Y, Z, TR, U = dims
    T = H * TR
    R = T * G
    PT = U * Y * Z * 2
    NPB = PT // KB
    NC = R // CB
    GC = CB // T
    scale = W**-0.5
    c2 = scale * math.log2(math.e)

    s_me = lax.axis_index("seq")
    h = lax.axis_index("head")
    c = s_me % 2
    z = (s_me // 2) % Z
    y = s_me // (2 * Z)

    def at(yy, zz, cc, hh):
        return {"seq": (yy * Z + zz) * 2 + cc, "head": hh}

    def rcopy(src, dst, ssem, rsem, dev):
        return pltpu.make_async_remote_copy(
            src_ref=src, dst_ref=dst, send_sem=ssem, recv_sem=rsem, device_id=dev, device_id_type=MESH
        )

    other = at(y, z, 1 - c, h)

    unit = jnp.concatenate([pk_ref[...].astype(F32), pv_ref[...].astype(F32)], axis=0)
    pg[c, y, z] = unit.astype(BF)

    barrier = pltpu.get_barrier_semaphore()
    for d in range(1, H):
        pl.semaphore_signal(barrier, inc=1, device_id=at(y, z, c, (h + d) % H), device_id_type=MESH)
    for d in range(1, Y):
        pl.semaphore_signal(barrier, inc=1, device_id=at((y + d) % Y, z, c, h), device_id_type=MESH)
    for d in range(1, Z):
        pl.semaphore_signal(barrier, inc=1, device_id=at(y, (z + d) % Z, c, h), device_id_type=MESH)
    pl.semaphore_signal(barrier, inc=1, device_id=other, device_id_type=MESH)
    pl.semaphore_wait(barrier, H + Y + Z - 2)

    my_blk = NPB + z
    my_rows = pl.multiple_of(c * T, T)
    GW = G * W

    def src_dst(a, t, rows):
        row = pl.ds(pl.multiple_of(rows * TR, TR), TR)
        kv_row = pl.ds(pl.multiple_of(c * T + rows * TR, TR), TR)
        wide = pl.ds(pl.multiple_of(t * GW, GW), GW)
        thin = pl.ds(pl.multiple_of(t * W, W), W)
        if a == 0:
            return k_hbm.at[:, thin], kvb.at[my_blk, 0, kv_row, :]
        if a == 1:
            return v_hbm.at[:, thin], kvb.at[my_blk, 1, kv_row, :]
        if a == 2:
            return q_hbm.at[:, wide], q_all.at[row, :]
        return do_hbm.at[:, wide], do_all.at[row, :]

    def a2a_copy(a, d):
        t = (h + d) % H
        src, dst = src_dst(a, t, h)
        return rcopy(src, dst, a2a_send.at[a, d], a2a_recv.at[a, d], at(y, z, c, t))

    def own_copy(a):
        src, dst = src_dst(a, h, h)
        return pltpu.make_async_copy(src, dst, own_sem.at[a])

    def a2a_start(a):
        own_copy(a).start()
        for d in range(1, H):
            a2a_copy(a, d).start()

    def a2a_wait(a):
        own_copy(a).wait()
        for d in range(1, H):
            frm = (h + H - d) % H
            src, dst = src_dst(a, h, frm)
            rcopy(src, dst, a2a_send.at[a, d], a2a_recv.at[a, d], at(y, z, c, frm)).wait_recv()

    a2a_start(0)
    a2a_start(1)

    def pz_copy(d):
        return rcopy(
            pg.at[c, y, z], pg.at[c, y, z], pz_send.at[d], pz_recv.at[d], at(y, (z + d) % Z, c, h)
        )

    def pz_from(d):
        f = (z + Z - d) % Z
        return rcopy(pg.at[c, y, f], pg.at[c, y, f], pz_send.at[d], pz_recv.at[d], at(y, f, c, h))

    for d in range(1, Z):
        pz_copy(d).start()
    a2a_start(2)
    for d in range(1, Z):
        pz_from(d).wait_recv()

    def py_copy(d):
        return rcopy(pg.at[c, y], pg.at[c, y], py_send.at[d], py_recv.at[d], at((y + d) % Y, z, c, h))

    def py_from(d):
        f = (y + Y - d) % Y
        return rcopy(pg.at[c, f], pg.at[c, f], py_send.at[d], py_recv.at[d], at(f, z, c, h))

    for d in range(1, Y):
        py_copy(d).start()

    a2a_wait(0)
    a2a_wait(1)

    def span_ref(zz, cc):
        return kvb.at[NPB + zz, :, pl.ds(pl.multiple_of(cc * T, T), T), :]

    def kz_copy(d):
        return rcopy(
            span_ref(z, c), span_ref(z, c), kz_send.at[d], kz_recv.at[d], at(y, z + d, c, h)
        )

    def kz_from(d):
        return rcopy(
            span_ref(z - d, c), span_ref(z - d, c), kz_send.at[d], kz_recv.at[d], at(y, z - d, c, h)
        )

    def kc_copy(d):
        return rcopy(span_ref(z - d, c), span_ref(z - d, c), kc_send.at[d], kc_recv.at[d], other)

    def kc_from(d):
        return rcopy(
            span_ref(z - d, 1 - c), span_ref(z - d, 1 - c), kc_send.at[d], kc_recv.at[d], other
        )

    for d in range(1, Z):

        @pl.when(z + d < Z)
        def _():
            kz_copy(d).start()

    kc_copy(0).start()
    a2a_start(3)

    for d in range(1, Y):
        py_from(d).wait_recv()

    def pc_copy(cc):
        return rcopy(pg.at[cc], pg.at[cc], pc_send, pc_recv, other)

    pc_copy(c).start()

    for d in range(1, Z):

        @pl.when(z - d >= 0)
        def _():
            kz_from(d).wait_recv()
            kc_copy(d).start()

    a2a_wait(2)
    for g in range(G):
        qr[g * T : (g + 1) * T, :] = q_all[:, g * W : (g + 1) * W]

    pc_copy(1 - c).wait_recv()
    units = []
    for s in range(Y * Z * 2):
        units.append(pg[s % 2, s // (2 * Z), (s // 2) % Z].astype(F32))
    per = KB // U
    for b in range(NPB):
        part = units[b * per : (b + 1) * per]
        kvb[b, 0] = jnp.concatenate([u[:U] for u in part], axis=0).astype(BF)
        kvb[b, 1] = jnp.concatenate([u[U:] for u in part], axis=0).astype(BF)

    kc_copy(0).wait_send()
    kc_from(0).wait_recv()
    for d in range(1, Z):

        @pl.when(z - d >= 0)
        def _():
            kc_from(d).wait_recv()

    nb = NPB + z + 1
    mx[...] = jnp.full_like(mx, NEG)

    def score_body(b, carry):
        keys = kvb[b, 0]
        kvt[b, 0] = keys.T
        kvt[b, 1] = kvb[b, 1].T
        edge = jnp.where(b == nb - 1, c * T, 1 << 20)
        rel = lax.broadcasted_iota(jnp.int32, (KB, T), 0) - lax.broadcasted_iota(jnp.int32, (KB, T), 1)
        seen = jnp.concatenate([rel <= edge] * GC, axis=1)
        for n in range(NC):
            cols = slice(n * CB, (n + 1) * CB)
            s = dot_nt(keys, qr[cols, :])
            s = jnp.where(seen, s, NEG)
            s_scr[b, :, cols] = s
            mx[:, cols] = jnp.maximum(mx[:, cols], jnp.max(s.reshape(KB // 8, 8, CB), axis=0))
        return carry

    lax.fori_loop(0, nb, score_body, 0)
    top = jnp.max(mx[...], axis=0, keepdims=True) * c2
    lx[...] = jnp.zeros_like(lx)
    o_acc[...] = jnp.zeros_like(o_acc)

    def weight_body(b, carry):
        vt = kvt[b, 1]
        for n in range(NC):
            cols = slice(n * CB, (n + 1) * CB)
            e = jnp.exp2(s_scr[b, :, cols] * c2 - top[:, cols])
            lx[:, cols] += jnp.sum(e.reshape(KB // 8, 8, CB), axis=0)
            p = e.astype(BF)
            p_scr[b, :, cols] = p
            o_acc[:, cols] += dot_nn(vt, p)
        return carry

    lax.fori_loop(0, nb, weight_body, 0)
    inv = 1.0 / jnp.sum(lx[...], axis=0, keepdims=True)

    length = len_ref[y]
    first = (2 * z + c) * T
    live_col = first + lax.broadcasted_iota(jnp.int32, (W, T), 1) < length
    live_row = first + lax.broadcasted_iota(jnp.int32, (T, W), 0) < length

    a2a_wait(3)
    deltas = []
    for g in range(G):
        rows = slice(g * T, (g + 1) * T)
        out_t = jnp.where(live_col, o_acc[:, rows] * inv[:, rows], 0.0).astype(BF)
        att_ref[:, g * W : (g + 1) * W] = out_t.T
        grad = jnp.where(live_row, do_all[:, g * W : (g + 1) * W].astype(F32), 0.0)
        dor[rows, :] = grad.astype(BF)
        grad_t = grad.T
        dot_t[:, rows] = grad_t.astype(BF)
        deltas.append(jnp.sum(grad_t * out_t.astype(F32), axis=0, keepdims=True))
    delta = jnp.concatenate(deltas, axis=1)
    dq_acc[...] = jnp.zeros_like(dq_acc)

    def gx_copy(p):
        return rcopy(xs.at[p, 1 - c], xr.at[p], gx_send.at[p], gx_recv.at[p], other)

    def gz_copy(p):
        return rcopy(zs.at[p], zr.at[z - p], gz_send.at[p], gz_recv.at[z - p], at(y, p, c, h))

    def gz_from(d):
        return rcopy(zs.at[z], zr.at[d], gz_send.at[z], gz_recv.at[d], at(y, z + d, c, h))

    def rc_copy():
        return rcopy(prom_s.at[1 - c], prom_r, rc_send, rc_recv, other)

    def ry_copy(d):
        t = (y + d) % Y
        return rcopy(prom_s.at[c, t], prom_y.at[d], ry_send.at[d], ry_recv.at[d], at(t, z, c, h))

    def rz_copy(d):
        t = (z + d) % Z
        return rcopy(prom_y.at[0, t], prom_z.at[d], rz_send.at[d], rz_recv.at[d], at(y, t, c, h))

    def grad_body(b, carry):
        values = kvb[b, 1]
        kt = kvt[b, 0]
        for n in range(NC):
            cols = slice(n * CB, (n + 1) * CB)
            dp = dot_nn(values, dot_t[:, cols])
            w = p_scr[b, :, cols].astype(F32) * inv[:, cols]
            ds = (w * (dp - delta[:, cols])).astype(BF)
            dv = dot_nn(w.astype(BF), dor[cols, :])
            dk = dot_nn(ds, qr[cols, :])
            dq_acc[:, cols] += dot_nn(kt, ds)
            if n == 0:
                acc[0] = dk
                acc[1] = dv
            else:
                acc[0] += dk
                acc[1] += dv

        per_y = Z * 2

        for blk in range(NPB):

            @pl.when(b == blk)
            def _():
                for i in range(KB // U):
                    s = blk * (KB // U) + i
                    rows = slice(i * U, (i + 1) * U)
                    both = jnp.concatenate([acc[0, rows, :] * scale, acc[1, rows, :]], axis=0)
                    prom_s[s % 2, s // per_y, (s // 2) % Z] = both.astype(BF)

        @pl.when(b == NPB - 1)
        def _():
            rc_copy().start()

        @pl.when(b >= NPB)
        def _():
            p = b - NPB
            for half in range(2):
                rows = slice(half * T, (half + 1) * T)
                xs[p, half, 0] = (acc[0, rows, :] * scale).astype(BF)
                xs[p, half, 1] = acc[1, rows, :].astype(BF)
            gx_copy(p).start()

        @pl.when(b == NPB)
        def _():
            rc_copy().wait()
            prom_s[c] = (prom_s[c].astype(F32) + prom_r[...].astype(F32)).astype(BF)
            for d in range(1, Y):
                ry_copy(d).start()

        @pl.when(b > NPB)
        def _():
            p = b - NPB - 1
            gx_copy(p).wait()
            zs[p] = (xs[p, c].astype(F32) + xr[p].astype(F32)).astype(BF)
            gz_copy(p).start()

        return carry

    lax.fori_loop(0, nb, grad_body, 0)

    for g in range(G):
        rows = slice(g * T, (g + 1) * T)
        dq_ref[:, g * W : (g + 1) * W] = (dq_acc[:, rows] * scale).T.astype(BF)

    total = prom_s[c, y].astype(F32)
    for d in range(1, Y):
        ry_copy(d).wait_recv()
        total += prom_y[d].astype(F32)
    prom_y[0] = total.astype(BF)
    for d in range(1, Z):
        rz_copy(d).start()

    gx_copy(z).wait()
    mine = xs[z, c].astype(F32) + xr[z].astype(F32)
    acc2 = acc
    acc2[0, :T] = mine[0]
    acc2[1, :T] = mine[1]
    for d in range(1, Z):

        @pl.when(z + d < Z)
        def _():
            gz_from(d).wait_recv()
            acc2[0, :T] += zr[d, 0].astype(F32)
            acc2[1, :T] += zr[d, 1].astype(F32)

    dkv_ref[0] = acc2[0, :T].astype(BF)
    dkv_ref[1] = acc2[1, :T].astype(BF)

    last = prom_y[0, z].astype(F32)
    for d in range(1, Z):
        rz_copy(d).wait_recv()
        last += prom_z[d].astype(F32)
    prom_ref[...] = last

    for a in range(4):
        for d in range(1, H):
            a2a_copy(a, d).wait_send()
    for d in range(1, Z):
        pz_copy(d).wait_send()
        rz_copy(d).wait_send()
    for d in range(1, Y):
        py_copy(d).wait_send()
        ry_copy(d).wait_send()
    pc_copy(c).wait_send()
    for d in range(1, Z):

        @pl.when(z + d < Z)
        def _():
            kz_copy(d).wait_send()

        @pl.when(z - d >= 0)
        def _():
            kc_copy(d).wait_send()
            gz_copy(z - d).wait_send()


def solution(mesh):
    H = mesh.shape["head"]
    S = mesh.shape["seq"]

    def per_device(q, rk, rv, pk, pv, do, lengths):
        TR = q.shape[0]
        T = TR * H
        Y = lengths.shape[0]
        Z = S // Y // 2
        U = pk.shape[0]
        R = T * G
        NB = U * S // KB + Z
        dims = (H, Y, Z, TR, U)
        dma = pltpu.SemaphoreType.DMA
        vm = pltpu.VMEM
        any_spec = pl.BlockSpec(memory_space=pl.ANY)
        vm_spec = pl.BlockSpec(memory_space=pltpu.VMEM)
        att, dq, dkv, prom = pl.pallas_call(
            functools.partial(kernel, dims),
            out_shape=[
                jax.ShapeDtypeStruct((T, G * W), BF),
                jax.ShapeDtypeStruct((T, G * W), BF),
                jax.ShapeDtypeStruct((2, T, W), BF),
                jax.ShapeDtypeStruct((2 * U, W), F32),
            ],
            in_specs=[
                any_spec,
                any_spec,
                any_spec,
                vm_spec,
                vm_spec,
                any_spec,
                pl.BlockSpec(memory_space=pltpu.SMEM),
            ],
            out_specs=[vm_spec] * 4,
            scratch_shapes=[
                vm((T, G * W), BF),
                vm((T, G * W), BF),
                vm((NB, 2, KB, W), BF),
                vm((NB, 2, W, KB), BF),
                vm((2, Y, Z, 2 * U, W), BF),
                vm((R, W), BF),
                vm((R, W), BF),
                vm((W, R), BF),
                vm((NB, KB, R), F32),
                vm((NB, KB, R), BF),
                vm((8, R), F32),
                vm((8, R), F32),
                vm((W, R), F32),
                vm((W, R), F32),
                vm((2, KB, W), F32),
                vm((2, Y, Z, 2 * U, W), BF),
                vm((Y, Z, 2 * U, W), BF),
                vm((Y, Z, 2 * U, W), BF),
                vm((Z, 2 * U, W), BF),
                vm((Z, 2, 2, T, W), BF),
                vm((Z, 2, T, W), BF),
                vm((Z, 2, T, W), BF),
                vm((Z, 2, T, W), BF),
                dma((4, H)),
                dma((4, H)),
                dma((4,)),
                dma((Z,)),
                dma((Z,)),
                dma((Y,)),
                dma((Y,)),
                dma,
                dma,
                dma((Z,)),
                dma((Z,)),
                dma((Z,)),
                dma((Z,)),
                dma((Z,)),
                dma((Z,)),
                dma((Z,)),
                dma((Z,)),
                dma,
                dma,
                dma((Y,)),
                dma((Y,)),
                dma((Z,)),
                dma((Z,)),
            ],
            compiler_params=pltpu.CompilerParams(
                collective_id=0, has_side_effects=True, vmem_limit_bytes=48 * 1024 * 1024
            ),
        )(q, rk, rv, pk, pv, do, lengths)
        return att, dq, dkv[0], dkv[1], prom[:U], prom[U:]

    tok = P(("seq", "head"), None)
    par = P("seq", "head")
    return jax.shard_map(
        per_device,
        mesh=mesh,
        in_specs=(tok, tok, tok, par, par, tok, P()),
        out_specs=(par,) * 6,
        check_vma=False,
    )
```

```python
import functools
import math

import jax
import jax.numpy as jnp
from jax import lax
from jax.experimental import pallas as pl
from jax.experimental.pallas import tpu as pltpu
from jax.sharding import PartitionSpec as P

MESH = pl.DeviceIdType.MESH
BF = jnp.bfloat16
F32 = jnp.float32
W = 128
G = 8
KB = 256
CB = 256
NEG = -1e30


def dot_nt(a, b):
    return lax.dot_general(a, b, (((1,), (1,)), ((), ())), preferred_element_type=F32)


def dot_nn(a, b):
    return lax.dot_general(a, b, (((1,), (0,)), ((), ())), preferred_element_type=F32)


def kernel(
    dims,
    q_hbm,
    k_hbm,
    v_hbm,
    pk_hbm,
    pv_hbm,
    do_hbm,
    len_hbm,
    att_ref,
    dq_ref,
    dk_ref,
    dv_ref,
    pdk_ref,
    pdv_ref,
    pk_ref,
    pv_ref,
    len_ref,
    small_sem,
    out_sem,
    att_v,
    dq_v,
    dk_v,
    dv_v,
    pdk_v,
    pdv_v,
    q_all,
    do_all,
    kvb,
    kvt,
    pg,
    qr,
    dor,
    dot_t,
    s_scr,
    p_scr,
    mx,
    lx,
    o_acc,
    dq_acc,
    acc,
    prom_s,
    prom_r,
    prom_y,
    prom_z,
    xs,
    xr,
    zs,
    zr,
    a2a_send,
    a2a_recv,
    own_sem,
    pz_send,
    pz_recv,
    py_send,
    py_recv,
    pc_send,
    pc_recv,
    kz_send,
    kz_recv,
    kc_send,
    kc_recv,
    gx_send,
    gx_recv,
    gz_send,
    gz_recv,
    rc_send,
    rc_recv,
    ry_send,
    ry_recv,
    rz_send,
    rz_recv,
):
    H, Y, Z, TR, U = dims
    T = H * TR
    R = T * G
    PT = U * Y * Z * 2
    NPB = PT // KB
    NC = R // CB
    GC = CB // T
    scale = W**-0.5
    c2 = scale * math.log2(math.e)

    s_me = lax.axis_index("seq")
    h = lax.axis_index("head")
    c = s_me % 2
    z = (s_me // 2) % Z
    y = s_me // (2 * Z)

    def at(yy, zz, cc, hh):
        return {"seq": (yy * Z + zz) * 2 + cc, "head": hh}

    def rcopy(src, dst, ssem, rsem, dev):
        return pltpu.make_async_remote_copy(
            src_ref=src, dst_ref=dst, send_sem=ssem, recv_sem=rsem, device_id=dev, device_id_type=MESH
        )

    other = at(y, z, 1 - c, h)

    small = [
        pltpu.make_async_copy(pk_hbm, pk_ref, small_sem.at[0]),
        pltpu.make_async_copy(pv_hbm, pv_ref, small_sem.at[1]),
        pltpu.make_async_copy(len_hbm, len_ref, small_sem.at[2]),
    ]
    for copy in small:
        copy.start()

    barrier = pltpu.get_barrier_semaphore()
    for d in range(1, H):
        pl.semaphore_signal(barrier, inc=1, device_id=at(y, z, c, (h + d) % H), device_id_type=MESH)
    for d in range(1, Y):
        pl.semaphore_signal(barrier, inc=1, device_id=at((y + d) % Y, z, c, h), device_id_type=MESH)
    for d in range(1, Z):
        pl.semaphore_signal(barrier, inc=1, device_id=at(y, (z + d) % Z, c, h), device_id_type=MESH)
    pl.semaphore_signal(barrier, inc=1, device_id=other, device_id_type=MESH)
    pl.semaphore_wait(barrier, H + Y + Z - 2)

    my_blk = NPB + z
    my_rows = pl.multiple_of(c * T, T)
    GW = G * W

    def src_dst(a, t, rows):
        row = pl.ds(pl.multiple_of(rows * TR, TR), TR)
        kv_row = pl.ds(pl.multiple_of(c * T + rows * TR, TR), TR)
        wide = pl.ds(pl.multiple_of(t * GW, GW), GW)
        thin = pl.ds(pl.multiple_of(t * W, W), W)
        if a == 0:
            return k_hbm.at[:, thin], kvb.at[my_blk, 0, kv_row, :]
        if a == 1:
            return v_hbm.at[:, thin], kvb.at[my_blk, 1, kv_row, :]
        if a == 2:
            return q_hbm.at[:, wide], q_all.at[row, :]
        return do_hbm.at[:, wide], do_all.at[row, :]

    def a2a_copy(a, d):
        t = (h + d) % H
        src, dst = src_dst(a, t, h)
        return rcopy(src, dst, a2a_send.at[a, d], a2a_recv.at[a, d], at(y, z, c, t))

    def own_copy(a):
        src, dst = src_dst(a, h, h)
        return pltpu.make_async_copy(src, dst, own_sem.at[a])

    def a2a_start(a):
        own_copy(a).start()
        for d in range(1, H):
            a2a_copy(a, d).start()

    def a2a_wait(a):
        own_copy(a).wait()
        for d in range(1, H):
            frm = (h + H - d) % H
            src, dst = src_dst(a, h, frm)
            rcopy(src, dst, a2a_send.at[a, d], a2a_recv.at[a, d], at(y, z, c, frm)).wait_recv()

    a2a_start(0)
    a2a_start(1)

    for copy in small:
        copy.wait()
    unit = jnp.concatenate([pk_ref[...].astype(F32), pv_ref[...].astype(F32)], axis=0)
    pg[c, y, z] = unit.astype(BF)

    def pz_copy(d):
        return rcopy(
            pg.at[c, y, z], pg.at[c, y, z], pz_send.at[d], pz_recv.at[d], at(y, (z + d) % Z, c, h)
        )

    def pz_from(d):
        f = (z + Z - d) % Z
        return rcopy(pg.at[c, y, f], pg.at[c, y, f], pz_send.at[d], pz_recv.at[d], at(y, f, c, h))

    for d in range(1, Z):
        pz_copy(d).start()
    a2a_start(2)

    def py_copy(d):
        return rcopy(pg.at[c, y], pg.at[c, y], py_send.at[d], py_recv.at[d], at((y + d) % Y, z, c, h))

    def py_from(d):
        f = (y + Y - d) % Y
        return rcopy(pg.at[c, f], pg.at[c, f], py_send.at[d], py_recv.at[d], at(f, z, c, h))

    def span_ref(zz, cc):
        return kvb.at[NPB + zz, :, pl.ds(pl.multiple_of(cc * T, T), T), :]

    def kz_copy(d):
        return rcopy(
            span_ref(z, c), span_ref(z, c), kz_send.at[d], kz_recv.at[d], at(y, z + d, c, h)
        )

    def kz_from(d):
        return rcopy(
            span_ref(z - d, c), span_ref(z - d, c), kz_send.at[d], kz_recv.at[d], at(y, z - d, c, h)
        )

    def kc_copy(d):
        return rcopy(span_ref(z - d, c), span_ref(z - d, c), kc_send.at[d], kc_recv.at[d], other)

    def kc_from(d):
        return rcopy(
            span_ref(z - d, 1 - c), span_ref(z - d, 1 - c), kc_send.at[d], kc_recv.at[d], other
        )

    def pc_copy(cc):
        return rcopy(pg.at[cc], pg.at[cc], pc_send, pc_recv, other)

    a2a_wait(0)
    a2a_wait(1)
    for d in range(1, Z):

        @pl.when(z + d < Z)
        def _():
            kz_copy(d).start()

    kc_copy(0).start()
    for d in range(1, Z):
        pz_from(d).wait_recv()
    for d in range(1, Y):
        py_copy(d).start()
    a2a_start(3)

    nb = NPB + z + 1
    mx[...] = jnp.full_like(mx, NEG)

    def scores(b):
        keys = kvb[b, 0]
        kvt[b, 0] = keys.T
        kvt[b, 1] = kvb[b, 1].T
        edge = jnp.where(b == nb - 1, c * T, 1 << 20)
        rel = lax.broadcasted_iota(jnp.int32, (KB, T), 0) - lax.broadcasted_iota(jnp.int32, (KB, T), 1)
        seen = jnp.concatenate([rel <= edge] * GC, axis=1)
        for n in range(NC):
            cols = slice(n * CB, (n + 1) * CB)
            s = dot_nt(keys, qr[cols, :])
            s = jnp.where(seen, s, NEG)
            s_scr[b, :, cols] = s
            mx[:, cols] = jnp.maximum(mx[:, cols], jnp.max(s.reshape(KB // 8, 8, CB), axis=0))

    a2a_wait(2)
    for g in range(G):
        qr[g * T : (g + 1) * T, :] = q_all[:, g * W : (g + 1) * W]
    for d in range(1, Y):
        py_from(d).wait_recv()
    pc_copy(c).start()
    for d in range(1, Z):

        @pl.when(z - d >= 0)
        def _():
            kz_from(d).wait_recv()
            kc_copy(d).start()

    pc_copy(1 - c).wait_recv()
    units = []
    for s in range(Y * Z * 2):
        units.append(pg[s % 2, s // (2 * Z), (s // 2) % Z].astype(F32))
    per = KB // U
    for b in range(NPB):
        part = units[b * per : (b + 1) * per]
        kvb[b, 0] = jnp.concatenate([u[:U] for u in part], axis=0).astype(BF)
        kvb[b, 1] = jnp.concatenate([u[U:] for u in part], axis=0).astype(BF)

    kc_copy(0).wait_send()
    kc_from(0).wait_recv()
    for d in range(1, Z):

        @pl.when(z - d >= 0)
        def _():
            kc_from(d).wait_recv()

    def score_body(b, carry):
        scores(b)
        return carry

    lax.fori_loop(0, nb, score_body, 0)
    top = jnp.max(mx[...], axis=0, keepdims=True) * c2
    lx[...] = jnp.zeros_like(lx)
    o_acc[...] = jnp.zeros_like(o_acc)

    def weight_body(b, carry):
        vt = kvt[b, 1]
        for n in range(NC):
            cols = slice(n * CB, (n + 1) * CB)
            e = jnp.exp2(s_scr[b, :, cols] * c2 - top[:, cols])
            lx[:, cols] += jnp.sum(e.reshape(KB // 8, 8, CB), axis=0)
            p = e.astype(BF)
            p_scr[b, :, cols] = p
            o_acc[:, cols] += dot_nn(vt, p)
        return carry

    lax.fori_loop(0, nb, weight_body, 0)
    inv = 1.0 / jnp.sum(lx[...], axis=0, keepdims=True)

    length = len_ref[y]
    first = (2 * z + c) * T
    live_col = first + lax.broadcasted_iota(jnp.int32, (W, T), 1) < length
    live_row = first + lax.broadcasted_iota(jnp.int32, (T, W), 0) < length

    for g in range(G):
        rows = slice(g * T, (g + 1) * T)
        out_t = jnp.where(live_col, o_acc[:, rows] * inv[:, rows], 0.0)
        att_v[:, g * W : (g + 1) * W] = out_t.T.astype(BF)
        o_acc[:, rows] = out_t.astype(BF).astype(F32)
    att_out = pltpu.make_async_copy(att_v, att_ref, out_sem.at[0])
    att_out.start()

    a2a_wait(3)
    deltas = []
    for g in range(G):
        rows = slice(g * T, (g + 1) * T)
        grad = jnp.where(live_row, do_all[:, g * W : (g + 1) * W].astype(F32), 0.0)
        dor[rows, :] = grad.astype(BF)
        grad_t = grad.T
        dot_t[:, rows] = grad_t.astype(BF)
        deltas.append(jnp.sum(grad_t * o_acc[:, rows], axis=0, keepdims=True))
    delta = jnp.concatenate(deltas, axis=1)
    dq_acc[...] = jnp.zeros_like(dq_acc)

    def gx_copy(p):
        return rcopy(xs.at[p, 1 - c], xr.at[p], gx_send.at[p], gx_recv.at[p], other)

    def gz_copy(p):
        return rcopy(zs.at[p], zr.at[z - p], gz_send.at[p], gz_recv.at[z - p], at(y, p, c, h))

    def gz_from(d):
        return rcopy(zs.at[z], zr.at[d], gz_send.at[z], gz_recv.at[d], at(y, z + d, c, h))

    def rc_copy():
        return rcopy(prom_s.at[1 - c], prom_r, rc_send, rc_recv, other)

    def ry_copy(d):
        t = (y + d) % Y
        return rcopy(prom_s.at[c, t], prom_y.at[d], ry_send.at[d], ry_recv.at[d], at(t, z, c, h))

    def rz_copy(d):
        t = (z + d) % Z
        return rcopy(prom_y.at[0, t], prom_z.at[d], rz_send.at[d], rz_recv.at[d], at(y, t, c, h))

    def grad_body(b, carry):
        values = kvb[b, 1]
        kt = kvt[b, 0]
        for n in range(NC):
            cols = slice(n * CB, (n + 1) * CB)
            dp = dot_nn(values, dot_t[:, cols])
            w = p_scr[b, :, cols].astype(F32) * inv[:, cols]
            ds = (w * (dp - delta[:, cols])).astype(BF)
            dv = dot_nn(w.astype(BF), dor[cols, :])
            dk = dot_nn(ds, qr[cols, :])
            dq_acc[:, cols] += dot_nn(kt, ds)
            if n == 0:
                acc[0] = dk
                acc[1] = dv
            else:
                acc[0] += dk
                acc[1] += dv

        per_y = Z * 2

        for blk in range(NPB):

            @pl.when(b == blk)
            def _():
                for i in range(KB // U):
                    s = blk * (KB // U) + i
                    rows = slice(i * U, (i + 1) * U)
                    both = jnp.concatenate([acc[0, rows, :] * scale, acc[1, rows, :]], axis=0)
                    prom_s[s % 2, s // per_y, (s // 2) % Z] = both.astype(BF)

        @pl.when(b == NPB - 1)
        def _():
            rc_copy().start()

        @pl.when(b >= NPB)
        def _():
            p = b - NPB
            for half in range(2):
                rows = slice(half * T, (half + 1) * T)
                xs[p, half, 0] = (acc[0, rows, :] * scale).astype(BF)
                xs[p, half, 1] = acc[1, rows, :].astype(BF)
            gx_copy(p).start()

        @pl.when(b == NPB)
        def _():
            rc_copy().wait()
            prom_s[c] = (prom_s[c].astype(F32) + prom_r[...].astype(F32)).astype(BF)
            for d in range(1, Y):
                ry_copy(d).start()

        @pl.when(b > NPB)
        def _():
            p = b - NPB - 1
            gx_copy(p).wait()
            zs[p] = (xs[p, c].astype(F32) + xr[p].astype(F32)).astype(BF)
            gz_copy(p).start()

        return carry

    lax.fori_loop(0, nb, grad_body, 0)

    for g in range(G):
        rows = slice(g * T, (g + 1) * T)
        dq_v[:, g * W : (g + 1) * W] = (dq_acc[:, rows] * scale).T.astype(BF)
    dq_out = pltpu.make_async_copy(dq_v, dq_ref, out_sem.at[1])
    dq_out.start()

    total = prom_s[c, y].astype(F32)
    for d in range(1, Y):
        ry_copy(d).wait_recv()
        total += prom_y[d].astype(F32)
    prom_y[0] = total.astype(BF)
    for d in range(1, Z):
        rz_copy(d).start()

    gx_copy(z).wait()
    mine = xs[z, c].astype(F32) + xr[z].astype(F32)
    acc2 = acc
    acc2[0, :T] = mine[0]
    acc2[1, :T] = mine[1]
    for d in range(1, Z):

        @pl.when(z + d < Z)
        def _():
            gz_from(d).wait_recv()
            acc2[0, :T] += zr[d, 0].astype(F32)
            acc2[1, :T] += zr[d, 1].astype(F32)

    dk_v[...] = acc2[0, :T].astype(BF)
    dv_v[...] = acc2[1, :T].astype(BF)
    dk_out = pltpu.make_async_copy(dk_v, dk_ref, out_sem.at[2])
    dv_out = pltpu.make_async_copy(dv_v, dv_ref, out_sem.at[3])
    dk_out.start()
    dv_out.start()

    last = prom_y[0, z].astype(F32)
    for d in range(1, Z):
        rz_copy(d).wait_recv()
        last += prom_z[d].astype(F32)
    pdk_v[...] = last[:U]
    pdv_v[...] = last[U:]
    pdk_out = pltpu.make_async_copy(pdk_v, pdk_ref, out_sem.at[4])
    pdv_out = pltpu.make_async_copy(pdv_v, pdv_ref, out_sem.at[5])
    pdk_out.start()
    pdv_out.start()
    for copy in (att_out, dq_out, dk_out, dv_out, pdk_out, pdv_out):
        copy.wait()

    for a in range(4):
        for d in range(1, H):
            a2a_copy(a, d).wait_send()
    for d in range(1, Z):
        pz_copy(d).wait_send()
        rz_copy(d).wait_send()
    for d in range(1, Y):
        py_copy(d).wait_send()
        ry_copy(d).wait_send()
    pc_copy(c).wait_send()
    for d in range(1, Z):

        @pl.when(z + d < Z)
        def _():
            kz_copy(d).wait_send()

        @pl.when(z - d >= 0)
        def _():
            kc_copy(d).wait_send()
            gz_copy(z - d).wait_send()


def write_out(*refs):
    given, written, held, sems = refs[:6], refs[6:12], refs[12:18], refs[18]
    reads = [pltpu.make_async_copy(given[i], held[i], sems.at[0, i]) for i in range(6)]
    writes = [pltpu.make_async_copy(held[i], written[i], sems.at[1, i]) for i in range(6)]
    for copy in reads:
        copy.start()
    for i in range(6):
        reads[i].wait()
        writes[i].start()
    for copy in writes:
        copy.wait()


def solution(mesh):
    H = mesh.shape["head"]
    S = mesh.shape["seq"]

    def per_device(q, rk, rv, pk, pv, do, lengths):
        TR = q.shape[0]
        T = TR * H
        Y = lengths.shape[0]
        Z = S // Y // 2
        U = pk.shape[0]
        R = T * G
        NB = U * S // KB + Z
        dims = (H, Y, Z, TR, U)
        dma = pltpu.SemaphoreType.DMA
        vm = pltpu.VMEM
        any_spec = pl.BlockSpec(memory_space=pl.ANY)
        shapes = [
            jax.ShapeDtypeStruct((T, G * W), BF),
            jax.ShapeDtypeStruct((T, G * W), BF),
            jax.ShapeDtypeStruct((T, W), BF),
            jax.ShapeDtypeStruct((T, W), BF),
            jax.ShapeDtypeStruct((U, W), F32),
            jax.ShapeDtypeStruct((U, W), F32),
        ]
        results = pl.pallas_call(
            functools.partial(kernel, dims),
            out_shape=shapes,
            in_specs=[any_spec] * 7,
            out_specs=[any_spec] * 6,
            scratch_shapes=[
                vm((U, W), BF),
                vm((U, W), BF),
                pltpu.SMEM((Y,), jnp.int32),
                dma((3,)),
                dma((6,)),
            ]
            + [vm(x.shape, x.dtype) for x in shapes]
            + [
                vm((T, G * W), BF),
                vm((T, G * W), BF),
                vm((NB, 2, KB, W), BF),
                vm((NB, 2, W, KB), BF),
                vm((2, Y, Z, 2 * U, W), BF),
                vm((R, W), BF),
                vm((R, W), BF),
                vm((W, R), BF),
                vm((NB, KB, R), F32),
                vm((NB, KB, R), BF),
                vm((8, R), F32),
                vm((8, R), F32),
                vm((W, R), F32),
                vm((W, R), F32),
                vm((2, KB, W), F32),
                vm((2, Y, Z, 2 * U, W), BF),
                vm((Y, Z, 2 * U, W), BF),
                vm((Y, Z, 2 * U, W), BF),
                vm((Z, 2 * U, W), BF),
                vm((Z, 2, 2, T, W), BF),
                vm((Z, 2, T, W), BF),
                vm((Z, 2, T, W), BF),
                vm((Z, 2, T, W), BF),
                dma((4, H)),
                dma((4, H)),
                dma((4,)),
                dma((Z,)),
                dma((Z,)),
                dma((Y,)),
                dma((Y,)),
                dma,
                dma,
                dma((Z,)),
                dma((Z,)),
                dma((Z,)),
                dma((Z,)),
                dma((Z,)),
                dma((Z,)),
                dma((Z,)),
                dma((Z,)),
                dma,
                dma,
                dma((Y,)),
                dma((Y,)),
                dma((Z,)),
                dma((Z,)),
            ],
            compiler_params=pltpu.CompilerParams(
                collective_id=0, has_side_effects=True, vmem_limit_bytes=60 * 1024 * 1024
            ),
        )(q, rk, rv, pk, pv, do, lengths)
        return pl.pallas_call(
            write_out,
            out_shape=shapes,
            in_specs=[any_spec] * 6,
            out_specs=[any_spec] * 6,
            scratch_shapes=[vm(x.shape, x.dtype) for x in shapes] + [dma((2, 6))],
            compiler_params=pltpu.CompilerParams(vmem_limit_bytes=60 * 1024 * 1024),
        )(*results)

    tok = P(("seq", "head"), None)
    par = P("seq", "head")
    return jax.shard_map(
        per_device,
        mesh=mesh,
        in_specs=(tok, tok, tok, par, par, tok, P()),
        out_specs=(par,) * 6,
        check_vma=False,
    )
```

```python
import functools
import math

import jax
import jax.numpy as jnp
from jax import lax
from jax.experimental import pallas as pl
from jax.experimental.pallas import tpu as pltpu
from jax.sharding import PartitionSpec as P

MESH = pl.DeviceIdType.MESH
BF = jnp.bfloat16
F32 = jnp.float32
W = 128
G = 8
KB = 256
CB = 512
NEG = -1e30


def dot_nt(a, b):
    return lax.dot_general(a, b, (((1,), (1,)), ((), ())), preferred_element_type=F32)


def dot_nn(a, b):
    return lax.dot_general(a, b, (((1,), (0,)), ((), ())), preferred_element_type=F32)


def kernel(
    dims,
    q_hbm,
    k_hbm,
    v_hbm,
    pk_hbm,
    pv_hbm,
    do_hbm,
    len_hbm,
    att_ref,
    dq_ref,
    dk_ref,
    dv_ref,
    pdk_ref,
    pdv_ref,
    pk_ref,
    pv_ref,
    len_ref,
    kv_held,
    small_sem,
    out_sem,
    att_v,
    dq_v,
    dk_v,
    dv_v,
    pdk_v,
    pdv_v,
    q_all,
    do_all,
    kvb,
    kvt,
    pg,
    qr,
    dor,
    dot_t,
    s_scr,
    p_scr,
    mx,
    lx,
    o_acc,
    dq_acc,
    acc,
    prom_s,
    prom_r,
    prom_y,
    prom_z,
    xs,
    xr,
    zs,
    zr,
    a2a_send,
    a2a_recv,
    own_sem,
    pz_send,
    pz_recv,
    py_send,
    py_recv,
    pc_send,
    pc_recv,
    kz_send,
    kz_recv,
    kc_send,
    kc_recv,
    gx_send,
    gx_recv,
    gz_send,
    gz_recv,
    rc_send,
    rc_recv,
    ry_send,
    ry_recv,
    rz_send,
    rz_recv,
):
    H, Y, Z, TR, U = dims
    T = H * TR
    R = T * G
    PT = U * Y * Z * 2
    NPB = PT // KB
    NC = R // CB
    GC = CB // T
    scale = W**-0.5
    c2 = scale * math.log2(math.e)

    s_me = lax.axis_index("seq")
    h = lax.axis_index("head")
    c = s_me % 2
    z = (s_me // 2) % Z
    y = s_me // (2 * Z)

    def at(yy, zz, cc, hh):
        return {"seq": (yy * Z + zz) * 2 + cc, "head": hh}

    def rcopy(src, dst, ssem, rsem, dev):
        return pltpu.make_async_remote_copy(
            src_ref=src, dst_ref=dst, send_sem=ssem, recv_sem=rsem, device_id=dev, device_id_type=MESH
        )

    other = at(y, z, 1 - c, h)

    small = [
        pltpu.make_async_copy(pk_hbm, pk_ref, small_sem.at[0]),
        pltpu.make_async_copy(pv_hbm, pv_ref, small_sem.at[1]),
        pltpu.make_async_copy(len_hbm, len_ref, small_sem.at[2]),
        pltpu.make_async_copy(k_hbm, kv_held.at[0], small_sem.at[3]),
        pltpu.make_async_copy(v_hbm, kv_held.at[1], small_sem.at[4]),
    ]
    for copy in small:
        copy.start()

    barrier = pltpu.get_barrier_semaphore()
    for d in range(1, H):
        pl.semaphore_signal(barrier, inc=1, device_id=at(y, z, c, (h + d) % H), device_id_type=MESH)
    for d in range(1, Y):
        pl.semaphore_signal(barrier, inc=1, device_id=at((y + d) % Y, z, c, h), device_id_type=MESH)
    for d in range(1, Z):
        pl.semaphore_signal(barrier, inc=1, device_id=at(y, (z + d) % Z, c, h), device_id_type=MESH)
    pl.semaphore_signal(barrier, inc=1, device_id=other, device_id_type=MESH)
    pl.semaphore_wait(barrier, H + Y + Z - 2)

    my_blk = NPB + z
    my_rows = pl.multiple_of(c * T, T)
    GW = G * W

    def src_dst(a, t, rows):
        row = pl.ds(pl.multiple_of(rows * TR, TR), TR)
        kv_row = pl.ds(pl.multiple_of(c * T + rows * TR, TR), TR)
        wide = pl.ds(pl.multiple_of(t * GW, GW), GW)
        thin = pl.ds(pl.multiple_of(t * W, W), W)
        if a == 0:
            return kv_held.at[:, :, thin], kvb.at[my_blk, :, kv_row, :]
        if a == 1:
            return q_hbm.at[:, wide], q_all.at[row, :]
        return do_hbm.at[:, wide], do_all.at[row, :]

    def a2a_copy(a, d):
        t = (h + d) % H
        src, dst = src_dst(a, t, h)
        return rcopy(src, dst, a2a_send.at[a, d], a2a_recv.at[a, d], at(y, z, c, t))

    def own_copy(a):
        src, dst = src_dst(a, h, h)
        return pltpu.make_async_copy(src, dst, own_sem.at[a])

    def a2a_start(a):
        own_copy(a).start()
        for d in range(1, H):
            a2a_copy(a, d).start()

    def a2a_wait(a):
        own_copy(a).wait()
        for d in range(1, H):
            frm = (h + H - d) % H
            src, dst = src_dst(a, h, frm)
            rcopy(src, dst, a2a_send.at[a, d], a2a_recv.at[a, d], at(y, z, c, frm)).wait_recv()

    for copy in small:
        copy.wait()
    a2a_start(0)

    unit = jnp.concatenate([pk_ref[...].astype(F32), pv_ref[...].astype(F32)], axis=0)
    pg[c, y, z] = unit.astype(BF)

    def pz_copy(d):
        return rcopy(
            pg.at[c, y, z], pg.at[c, y, z], pz_send.at[d], pz_recv.at[d], at(y, (z + d) % Z, c, h)
        )

    def pz_from(d):
        f = (z + Z - d) % Z
        return rcopy(pg.at[c, y, f], pg.at[c, y, f], pz_send.at[d], pz_recv.at[d], at(y, f, c, h))

    for d in range(1, Z):
        pz_copy(d).start()
    a2a_start(1)

    def py_copy(d):
        return rcopy(pg.at[c, y], pg.at[c, y], py_send.at[d], py_recv.at[d], at((y + d) % Y, z, c, h))

    def py_from(d):
        f = (y + Y - d) % Y
        return rcopy(pg.at[c, f], pg.at[c, f], py_send.at[d], py_recv.at[d], at(f, z, c, h))

    def span_ref(zz, cc):
        return kvb.at[NPB + zz, :, pl.ds(pl.multiple_of(cc * T, T), T), :]

    def kz_copy(d):
        return rcopy(
            span_ref(z, c), span_ref(z, c), kz_send.at[d], kz_recv.at[d], at(y, z + d, c, h)
        )

    def kz_from(d):
        return rcopy(
            span_ref(z - d, c), span_ref(z - d, c), kz_send.at[d], kz_recv.at[d], at(y, z - d, c, h)
        )

    def kc_copy(d):
        return rcopy(span_ref(z - d, c), span_ref(z - d, c), kc_send.at[d], kc_recv.at[d], other)

    def kc_from(d):
        return rcopy(
            span_ref(z - d, 1 - c), span_ref(z - d, 1 - c), kc_send.at[d], kc_recv.at[d], other
        )

    def pc_copy(cc):
        return rcopy(pg.at[cc], pg.at[cc], pc_send, pc_recv, other)

    a2a_wait(0)
    for d in range(1, Z):

        @pl.when(z + d < Z)
        def _():
            kz_copy(d).start()

    kc_copy(0).start()
    for d in range(1, Z):
        pz_from(d).wait_recv()
    for d in range(1, Y):
        py_copy(d).start()
    a2a_start(2)

    nb = NPB + z + 1
    mx[...] = jnp.full_like(mx, NEG)

    def scores(b, edge):
        rel = lax.broadcasted_iota(jnp.int32, (KB, T), 0) - lax.broadcasted_iota(jnp.int32, (KB, T), 1)
        seen = jnp.concatenate([rel <= c * T] * GC, axis=1)
        keys = kvb[b, 0]
        kvt[b, 0] = keys.T
        kvt[b, 1] = kvb[b, 1].T
        for n in range(NC):
            cols = slice(n * CB, (n + 1) * CB)
            s = dot_nt(keys, qr[cols, :])
            if edge:
                s = jnp.where(seen, s, NEG)
            s_scr[b, :, cols] = s
            mx[:, cols] = jnp.maximum(mx[:, cols], jnp.max(s.reshape(KB // 8, 8, CB), axis=0))

    def score_body(b, carry):
        scores(b, False)
        return carry

    a2a_wait(1)
    for g in range(G):
        qr[g * T : (g + 1) * T, :] = q_all[:, g * W : (g + 1) * W]
    for d in range(1, Y):
        py_from(d).wait_recv()
    pc_copy(c).start()
    for d in range(1, Z):

        @pl.when(z - d >= 0)
        def _():
            kz_from(d).wait_recv()
            kc_copy(d).start()

    pc_copy(1 - c).wait_recv()
    units = []
    for s in range(Y * Z * 2):
        units.append(pg[s % 2, s // (2 * Z), (s // 2) % Z].astype(F32))
    per = KB // U
    for b in range(NPB):
        part = units[b * per : (b + 1) * per]
        kvb[b, 0] = jnp.concatenate([u[:U] for u in part], axis=0).astype(BF)
        kvb[b, 1] = jnp.concatenate([u[U:] for u in part], axis=0).astype(BF)

    kc_copy(0).wait_send()
    kc_from(0).wait_recv()
    scores(nb - 1, True)
    lax.fori_loop(0, NPB, score_body, 0)
    for d in range(1, Z):

        @pl.when(z - d >= 0)
        def _():
            kc_from(d).wait_recv()

    lax.fori_loop(NPB, nb - 1, score_body, 0)
    top = jnp.max(mx[...], axis=0, keepdims=True) * c2
    lx[...] = jnp.zeros_like(lx)
    o_acc[...] = jnp.zeros_like(o_acc)

    def weight_body(b, carry):
        vt = kvt[b, 1]
        for n in range(NC):
            cols = slice(n * CB, (n + 1) * CB)
            e = jnp.exp2(s_scr[b, :, cols] * c2 - top[:, cols])
            lx[:, cols] += jnp.sum(e.reshape(KB // 8, 8, CB), axis=0)
            p = e.astype(BF)
            p_scr[b, :, cols] = p
            o_acc[:, cols] += dot_nn(vt, p)
        return carry

    lax.fori_loop(0, nb, weight_body, 0)
    inv = 1.0 / jnp.sum(lx[...], axis=0, keepdims=True)

    length = len_ref[y]
    first = (2 * z + c) * T
    live_col = first + lax.broadcasted_iota(jnp.int32, (W, T), 1) < length
    live_row = first + lax.broadcasted_iota(jnp.int32, (T, W), 0) < length

    for g in range(G):
        rows = slice(g * T, (g + 1) * T)
        out_t = jnp.where(live_col, o_acc[:, rows] * inv[:, rows], 0.0)
        att_v[:, g * W : (g + 1) * W] = out_t.T.astype(BF)
        o_acc[:, rows] = out_t.astype(BF).astype(F32)
    att_out = pltpu.make_async_copy(att_v, att_ref, out_sem.at[0])
    att_out.start()

    a2a_wait(2)
    deltas = []
    for g in range(G):
        rows = slice(g * T, (g + 1) * T)
        grad = jnp.where(live_row, do_all[:, g * W : (g + 1) * W].astype(F32), 0.0)
        dor[rows, :] = grad.astype(BF)
        grad_t = grad.T
        dot_t[:, rows] = grad_t.astype(BF)
        deltas.append(jnp.sum(grad_t * o_acc[:, rows], axis=0, keepdims=True))
    delta = jnp.concatenate(deltas, axis=1)
    dq_acc[...] = jnp.zeros_like(dq_acc)

    def gx_copy(p):
        return rcopy(xs.at[p, 1 - c], xr.at[p], gx_send.at[p], gx_recv.at[p], other)

    def gz_copy(p):
        return rcopy(zs.at[p], zr.at[z - p], gz_send.at[p], gz_recv.at[z - p], at(y, p, c, h))

    def gz_from(d):
        return rcopy(zs.at[z], zr.at[d], gz_send.at[z], gz_recv.at[d], at(y, z + d, c, h))

    def rc_copy():
        return rcopy(prom_s.at[1 - c], prom_r, rc_send, rc_recv, other)

    def ry_copy(d):
        t = (y + d) % Y
        return rcopy(prom_s.at[c, t], prom_y.at[d], ry_send.at[d], ry_recv.at[d], at(t, z, c, h))

    def rz_copy(d):
        t = (z + d) % Z
        return rcopy(prom_y.at[0, t], prom_z.at[d], rz_send.at[d], rz_recv.at[d], at(y, t, c, h))

    def grad_body(b, carry):
        values = kvb[b, 1]
        kt = kvt[b, 0]
        for n in range(NC):
            cols = slice(n * CB, (n + 1) * CB)
            dp = dot_nn(values, dot_t[:, cols])
            w = p_scr[b, :, cols].astype(F32) * inv[:, cols]
            ds = (w * (dp - delta[:, cols])).astype(BF)
            dv = dot_nn(w.astype(BF), dor[cols, :])
            dk = dot_nn(ds, qr[cols, :])
            dq_acc[:, cols] += dot_nn(kt, ds)
            if n == 0:
                acc[0] = dk
                acc[1] = dv
            else:
                acc[0] += dk
                acc[1] += dv

        per_y = Z * 2

        for blk in range(NPB):

            @pl.when(b == blk)
            def _():
                for i in range(KB // U):
                    s = blk * (KB // U) + i
                    rows = slice(i * U, (i + 1) * U)
                    both = jnp.concatenate([acc[0, rows, :] * scale, acc[1, rows, :]], axis=0)
                    prom_s[s % 2, s // per_y, (s // 2) % Z] = both.astype(BF)

        @pl.when(b == NPB - 1)
        def _():
            rc_copy().start()

        @pl.when(b >= NPB)
        def _():
            p = b - NPB
            for half in range(2):
                rows = slice(half * T, (half + 1) * T)
                xs[p, half, 0] = (acc[0, rows, :] * scale).astype(BF)
                xs[p, half, 1] = acc[1, rows, :].astype(BF)
            gx_copy(p).start()

        @pl.when(b == NPB)
        def _():
            rc_copy().wait()
            prom_s[c] = (prom_s[c].astype(F32) + prom_r[...].astype(F32)).astype(BF)
            for d in range(1, Y):
                ry_copy(d).start()

        @pl.when(b > NPB)
        def _():
            p = b - NPB - 1
            gx_copy(p).wait()
            zs[p] = (xs[p, c].astype(F32) + xr[p].astype(F32)).astype(BF)
            gz_copy(p).start()

        return carry

    lax.fori_loop(0, nb, grad_body, 0)

    for g in range(G):
        rows = slice(g * T, (g + 1) * T)
        dq_v[:, g * W : (g + 1) * W] = (dq_acc[:, rows] * scale).T.astype(BF)
    dq_out = pltpu.make_async_copy(dq_v, dq_ref, out_sem.at[1])
    dq_out.start()

    total = prom_s[c, y].astype(F32)
    for d in range(1, Y):
        ry_copy(d).wait_recv()
        total += prom_y[d].astype(F32)
    prom_y[0] = total.astype(BF)
    for d in range(1, Z):
        rz_copy(d).start()

    gx_copy(z).wait()
    mine = xs[z, c].astype(F32) + xr[z].astype(F32)
    acc2 = acc
    acc2[0, :T] = mine[0]
    acc2[1, :T] = mine[1]
    for d in range(1, Z):

        @pl.when(z + d < Z)
        def _():
            gz_from(d).wait_recv()
            acc2[0, :T] += zr[d, 0].astype(F32)
            acc2[1, :T] += zr[d, 1].astype(F32)

    dk_v[...] = acc2[0, :T].astype(BF)
    dv_v[...] = acc2[1, :T].astype(BF)
    dk_out = pltpu.make_async_copy(dk_v, dk_ref, out_sem.at[2])
    dv_out = pltpu.make_async_copy(dv_v, dv_ref, out_sem.at[3])
    dk_out.start()
    dv_out.start()

    last = prom_y[0, z].astype(F32)
    for d in range(1, Z):
        rz_copy(d).wait_recv()
        last += prom_z[d].astype(F32)
    pdk_v[...] = last[:U]
    pdv_v[...] = last[U:]
    pdk_out = pltpu.make_async_copy(pdk_v, pdk_ref, out_sem.at[4])
    pdv_out = pltpu.make_async_copy(pdv_v, pdv_ref, out_sem.at[5])
    pdk_out.start()
    pdv_out.start()
    for copy in (att_out, dq_out, dk_out, dv_out, pdk_out, pdv_out):
        copy.wait()

    for a in range(3):
        for d in range(1, H):
            a2a_copy(a, d).wait_send()
    for d in range(1, Z):
        pz_copy(d).wait_send()
        rz_copy(d).wait_send()
    for d in range(1, Y):
        py_copy(d).wait_send()
        ry_copy(d).wait_send()
    pc_copy(c).wait_send()
    for d in range(1, Z):

        @pl.when(z + d < Z)
        def _():
            kz_copy(d).wait_send()

        @pl.when(z - d >= 0)
        def _():
            kc_copy(d).wait_send()
            gz_copy(z - d).wait_send()


def write_out(*refs):
    given, written, held, sems = refs[:6], refs[6:12], refs[12:18], refs[18]
    reads = [pltpu.make_async_copy(given[i], held[i], sems.at[0, i]) for i in range(6)]
    writes = [pltpu.make_async_copy(held[i], written[i], sems.at[1, i]) for i in range(6)]
    for copy in reads:
        copy.start()
    for i in range(6):
        reads[i].wait()
        writes[i].start()
    for copy in writes:
        copy.wait()


def solution(mesh):
    H = mesh.shape["head"]
    S = mesh.shape["seq"]

    def per_device(q, rk, rv, pk, pv, do, lengths):
        TR = q.shape[0]
        T = TR * H
        Y = lengths.shape[0]
        Z = S // Y // 2
        U = pk.shape[0]
        R = T * G
        NB = U * S // KB + Z
        dims = (H, Y, Z, TR, U)
        dma = pltpu.SemaphoreType.DMA
        vm = pltpu.VMEM
        any_spec = pl.BlockSpec(memory_space=pl.ANY)
        shapes = [
            jax.ShapeDtypeStruct((T, G * W), BF),
            jax.ShapeDtypeStruct((T, G * W), BF),
            jax.ShapeDtypeStruct((T, W), BF),
            jax.ShapeDtypeStruct((T, W), BF),
            jax.ShapeDtypeStruct((U, W), F32),
            jax.ShapeDtypeStruct((U, W), F32),
        ]
        results = pl.pallas_call(
            functools.partial(kernel, dims),
            out_shape=shapes,
            in_specs=[any_spec] * 7,
            out_specs=[any_spec] * 6,
            scratch_shapes=[
                vm((U, W), BF),
                vm((U, W), BF),
                pltpu.SMEM((Y,), jnp.int32),
                vm((2, TR, H * W), BF),
                dma((5,)),
                dma((6,)),
            ]
            + [vm(x.shape, x.dtype) for x in shapes]
            + [
                vm((T, G * W), BF),
                vm((T, G * W), BF),
                vm((NB, 2, KB, W), BF),
                vm((NB, 2, W, KB), BF),
                vm((2, Y, Z, 2 * U, W), BF),
                vm((R, W), BF),
                vm((R, W), BF),
                vm((W, R), BF),
                vm((NB, KB, R), F32),
                vm((NB, KB, R), BF),
                vm((8, R), F32),
                vm((8, R), F32),
                vm((W, R), F32),
                vm((W, R), F32),
                vm((2, KB, W), F32),
                vm((2, Y, Z, 2 * U, W), BF),
                vm((Y, Z, 2 * U, W), BF),
                vm((Y, Z, 2 * U, W), BF),
                vm((Z, 2 * U, W), BF),
                vm((Z, 2, 2, T, W), BF),
                vm((Z, 2, T, W), BF),
                vm((Z, 2, T, W), BF),
                vm((Z, 2, T, W), BF),
                dma((3, H)),
                dma((3, H)),
                dma((3,)),
                dma((Z,)),
                dma((Z,)),
                dma((Y,)),
                dma((Y,)),
                dma,
                dma,
                dma((Z,)),
                dma((Z,)),
                dma((Z,)),
                dma((Z,)),
                dma((Z,)),
                dma((Z,)),
                dma((Z,)),
                dma((Z,)),
                dma,
                dma,
                dma((Y,)),
                dma((Y,)),
                dma((Z,)),
                dma((Z,)),
            ],
            compiler_params=pltpu.CompilerParams(
                collective_id=0, has_side_effects=True, vmem_limit_bytes=60 * 1024 * 1024
            ),
        )(q, rk, rv, pk, pv, do, lengths)
        return pl.pallas_call(
            write_out,
            out_shape=shapes,
            in_specs=[any_spec] * 6,
            out_specs=[any_spec] * 6,
            scratch_shapes=[vm(x.shape, x.dtype) for x in shapes] + [dma((2, 6))],
            compiler_params=pltpu.CompilerParams(vmem_limit_bytes=60 * 1024 * 1024),
        )(*results)

    tok = P(("seq", "head"), None)
    par = P("seq", "head")
    return jax.shard_map(
        per_device,
        mesh=mesh,
        in_specs=(tok, tok, tok, par, par, tok, P()),
        out_specs=(par,) * 6,
        check_vma=False,
    )
```

```python
import functools
import math

import jax
import jax.numpy as jnp
from jax import lax
from jax.experimental import pallas as pl
from jax.experimental.pallas import tpu as pltpu
from jax.sharding import PartitionSpec as P

MESH = pl.DeviceIdType.MESH
BF = jnp.bfloat16
F32 = jnp.float32
W = 128
G = 8
KB = 256
CB = 512
NEG = -1e30


def dot_nt(a, b):
    return lax.dot_general(a, b, (((1,), (1,)), ((), ())), preferred_element_type=F32)


def dot_nn(a, b):
    return lax.dot_general(a, b, (((1,), (0,)), ((), ())), preferred_element_type=F32)


def kernel(
    dims,
    q_hbm,
    k_hbm,
    v_hbm,
    pk_hbm,
    pv_hbm,
    do_hbm,
    len_hbm,
    att_ref,
    dq_ref,
    dk_ref,
    dv_ref,
    pdk_ref,
    pdv_ref,
    pk_ref,
    pv_ref,
    len_ref,
    kv_held,
    small_sem,
    out_sem,
    att_v,
    dq_v,
    dk_v,
    dv_v,
    pdk_v,
    pdv_v,
    q_all,
    do_all,
    kvb,
    kvt,
    pg,
    qr,
    dor,
    dot_t,
    s_scr,
    p_scr,
    mx,
    lx,
    o_acc,
    dq_acc,
    acc,
    prom_s,
    prom_r,
    prom_y,
    prom_z,
    xs,
    xr,
    zs,
    zr,
    a2a_send,
    a2a_recv,
    own_sem,
    pz_send,
    pz_recv,
    py_send,
    py_recv,
    pc_send,
    pc_recv,
    kz_send,
    kz_recv,
    kc_send,
    kc_recv,
    gx_send,
    gx_recv,
    gz_send,
    gz_recv,
    rc_send,
    rc_recv,
    ry_send,
    ry_recv,
    rz_send,
    rz_recv,
):
    H, Y, Z, TR, U = dims
    T = H * TR
    R = T * G
    PT = U * Y * Z * 2
    NPB = PT // KB
    NC = R // CB
    GC = CB // T
    scale = W**-0.5
    c2 = scale * math.log2(math.e)

    s_me = lax.axis_index("seq")
    h = lax.axis_index("head")
    c = s_me % 2
    z = (s_me // 2) % Z
    y = s_me // (2 * Z)

    def at(yy, zz, cc, hh):
        return {"seq": (yy * Z + zz) * 2 + cc, "head": hh}

    def rcopy(src, dst, ssem, rsem, dev):
        return pltpu.make_async_remote_copy(
            src_ref=src, dst_ref=dst, send_sem=ssem, recv_sem=rsem, device_id=dev, device_id_type=MESH
        )

    other = at(y, z, 1 - c, h)

    small = [
        pltpu.make_async_copy(pk_hbm, pk_ref, small_sem.at[0]),
        pltpu.make_async_copy(pv_hbm, pv_ref, small_sem.at[1]),
        pltpu.make_async_copy(len_hbm, len_ref, small_sem.at[2]),
        pltpu.make_async_copy(k_hbm, kv_held.at[0], small_sem.at[3]),
        pltpu.make_async_copy(v_hbm, kv_held.at[1], small_sem.at[4]),
    ]
    for copy in small:
        copy.start()

    barrier = pltpu.get_barrier_semaphore()
    for d in range(1, H):
        pl.semaphore_signal(barrier, inc=1, device_id=at(y, z, c, (h + d) % H), device_id_type=MESH)
    for d in range(1, Y):
        pl.semaphore_signal(barrier, inc=1, device_id=at((y + d) % Y, z, c, h), device_id_type=MESH)
    for d in range(1, Z):
        pl.semaphore_signal(barrier, inc=1, device_id=at(y, (z + d) % Z, c, h), device_id_type=MESH)
    pl.semaphore_signal(barrier, inc=1, device_id=other, device_id_type=MESH)
    pl.semaphore_wait(barrier, H + Y + Z - 2)

    my_blk = NPB + z
    my_rows = pl.multiple_of(c * T, T)
    GW = G * W

    def src_dst(a, t, rows):
        row = pl.ds(pl.multiple_of(rows * TR, TR), TR)
        kv_row = pl.ds(pl.multiple_of(c * T + rows * TR, TR), TR)
        wide = pl.ds(pl.multiple_of(t * GW, GW), GW)
        thin = pl.ds(pl.multiple_of(t * W, W), W)
        if a == 0:
            return kv_held.at[:, :, thin], kvb.at[my_blk, :, kv_row, :]
        if a == 1:
            return q_hbm.at[:, wide], q_all.at[row, :]
        return do_hbm.at[:, wide], do_all.at[row, :]

    def a2a_copy(a, d):
        t = (h + d) % H
        src, dst = src_dst(a, t, h)
        return rcopy(src, dst, a2a_send.at[a, d], a2a_recv.at[a, d], at(y, z, c, t))

    def own_copy(a):
        src, dst = src_dst(a, h, h)
        return pltpu.make_async_copy(src, dst, own_sem.at[a])

    def a2a_start(a):
        own_copy(a).start()
        for d in range(1, H):
            a2a_copy(a, d).start()

    def a2a_wait(a):
        own_copy(a).wait()
        for d in range(1, H):
            frm = (h + H - d) % H
            src, dst = src_dst(a, h, frm)
            rcopy(src, dst, a2a_send.at[a, d], a2a_recv.at[a, d], at(y, z, c, frm)).wait_recv()

    for copy in small:
        copy.wait()
    a2a_start(0)

    unit = jnp.concatenate([pk_ref[...].astype(F32), pv_ref[...].astype(F32)], axis=0)
    pg[c, y, z] = unit.astype(BF)

    def pz_copy(d):
        return rcopy(
            pg.at[c, y, z], pg.at[c, y, z], pz_send.at[d], pz_recv.at[d], at(y, (z + d) % Z, c, h)
        )

    def pz_from(d):
        f = (z + Z - d) % Z
        return rcopy(pg.at[c, y, f], pg.at[c, y, f], pz_send.at[d], pz_recv.at[d], at(y, f, c, h))

    for d in range(1, Z):
        pz_copy(d).start()
    a2a_start(1)

    def py_copy(d):
        return rcopy(pg.at[c, y], pg.at[c, y], py_send.at[d], py_recv.at[d], at((y + d) % Y, z, c, h))

    def py_from(d):
        f = (y + Y - d) % Y
        return rcopy(pg.at[c, f], pg.at[c, f], py_send.at[d], py_recv.at[d], at(f, z, c, h))

    def span_ref(zz, cc):
        return kvb.at[NPB + zz, :, pl.ds(pl.multiple_of(cc * T, T), T), :]

    def kz_copy(d):
        return rcopy(
            span_ref(z, c), span_ref(z, c), kz_send.at[d], kz_recv.at[d], at(y, z + d, c, h)
        )

    def kz_from(d):
        return rcopy(
            span_ref(z - d, c), span_ref(z - d, c), kz_send.at[d], kz_recv.at[d], at(y, z - d, c, h)
        )

    def kc_copy(d):
        return rcopy(span_ref(z - d, c), span_ref(z - d, c), kc_send.at[d], kc_recv.at[d], other)

    def kc_from(d):
        return rcopy(
            span_ref(z - d, 1 - c), span_ref(z - d, 1 - c), kc_send.at[d], kc_recv.at[d], other
        )

    def pc_copy(cc):
        return rcopy(pg.at[cc], pg.at[cc], pc_send, pc_recv, other)

    a2a_wait(0)
    for d in range(1, Z):

        @pl.when(z + d < Z)
        def _():
            kz_copy(d).start()

    kc_copy(0).start()
    for d in range(1, Z):
        pz_from(d).wait_recv()
    for d in range(1, Y):
        py_copy(d).start()
    a2a_start(2)

    nb = NPB + z + 1
    mx[...] = jnp.full_like(mx, NEG)

    def scores(b, edge):
        rel = lax.broadcasted_iota(jnp.int32, (KB, T), 0) - lax.broadcasted_iota(jnp.int32, (KB, T), 1)
        seen = jnp.concatenate([rel <= c * T] * GC, axis=1)
        keys = kvb[b, 0]
        kvt[b, 0] = keys.T
        kvt[b, 1] = kvb[b, 1].T
        for n in range(NC):
            cols = slice(n * CB, (n + 1) * CB)
            s = dot_nt(keys, qr[cols, :])
            if edge:
                s = jnp.where(seen, s, NEG)
            s_scr[b, :, cols] = s
            mx[:, cols] = jnp.maximum(mx[:, cols], jnp.max(s.reshape(KB // 8, 8, CB), axis=0))

    def score_body(b, carry):
        scores(b, False)
        return carry

    a2a_wait(1)
    for g in range(G):
        qr[g * T : (g + 1) * T, :] = q_all[:, g * W : (g + 1) * W]
    for d in range(1, Y):
        py_from(d).wait_recv()
    pc_copy(c).start()
    for d in range(1, Z):

        @pl.when(z - d >= 0)
        def _():
            kz_from(d).wait_recv()
            kc_copy(d).start()

    pc_copy(1 - c).wait_recv()
    units = []
    for s in range(Y * Z * 2):
        units.append(pg[s % 2, s // (2 * Z), (s // 2) % Z].astype(F32))
    per = KB // U
    for b in range(NPB):
        part = units[b * per : (b + 1) * per]
        kvb[b, 0] = jnp.concatenate([u[:U] for u in part], axis=0).astype(BF)
        kvb[b, 1] = jnp.concatenate([u[U:] for u in part], axis=0).astype(BF)

    kc_copy(0).wait_send()
    kc_from(0).wait_recv()
    scores(nb - 1, True)
    lax.fori_loop(0, NPB, score_body, 0)
    for d in range(1, Z):

        @pl.when(z - d >= 0)
        def _():
            kc_from(d).wait_recv()

    lax.fori_loop(NPB, nb - 1, score_body, 0)
    top = jnp.max(mx[...], axis=0, keepdims=True) * c2
    lx[...] = jnp.zeros_like(lx)
    o_acc[...] = jnp.zeros_like(o_acc)

    def weight_body(b, carry):
        vt = kvt[b, 1]
        for n in range(NC):
            cols = slice(n * CB, (n + 1) * CB)
            e = jnp.exp2(s_scr[b, :, cols] * c2 - top[:, cols])
            lx[:, cols] += jnp.sum(e.reshape(KB // 8, 8, CB), axis=0)
            p = e.astype(BF)
            p_scr[b, :, cols] = p
            o_acc[:, cols] += dot_nn(vt, p)
        return carry

    lax.fori_loop(0, nb, weight_body, 0)
    inv = 1.0 / jnp.sum(lx[...], axis=0, keepdims=True)

    length = len_ref[y]
    first = (2 * z + c) * T
    live_col = first + lax.broadcasted_iota(jnp.int32, (W, T), 1) < length
    live_row = first + lax.broadcasted_iota(jnp.int32, (T, W), 0) < length

    for g in range(G):
        rows = slice(g * T, (g + 1) * T)
        out_t = jnp.where(live_col, o_acc[:, rows] * inv[:, rows], 0.0)
        att_v[:, g * W : (g + 1) * W] = out_t.T.astype(BF)
        o_acc[:, rows] = out_t.astype(BF).astype(F32)
    att_out = pltpu.make_async_copy(att_v, att_ref, out_sem.at[0])
    att_out.start()

    a2a_wait(2)
    deltas = []
    for g in range(G):
        rows = slice(g * T, (g + 1) * T)
        grad = jnp.where(live_row, do_all[:, g * W : (g + 1) * W].astype(F32), 0.0)
        dor[rows, :] = grad.astype(BF)
        grad_t = grad.T
        dot_t[:, rows] = grad_t.astype(BF)
        deltas.append(jnp.sum(grad_t * o_acc[:, rows], axis=0, keepdims=True))
    delta = jnp.concatenate(deltas, axis=1)
    dq_acc[...] = jnp.zeros_like(dq_acc)

    def gx_copy(p):
        return rcopy(xs.at[p, 1 - c], xr.at[p], gx_send.at[p], gx_recv.at[p], other)

    def gz_copy(p):
        return rcopy(zs.at[p], zr.at[z - p], gz_send.at[p], gz_recv.at[z - p], at(y, p, c, h))

    def gz_from(d):
        return rcopy(zs.at[z], zr.at[d], gz_send.at[z], gz_recv.at[d], at(y, z + d, c, h))

    YB = Y // NPB

    def rc_copy(k):
        ys = pl.ds(k * YB, YB)
        return rcopy(prom_s.at[1 - c, ys], prom_r.at[ys], rc_send.at[k], rc_recv.at[k], other)

    def ry_copy(d):
        t = (y + d) % Y
        return rcopy(prom_s.at[c, t], prom_y.at[d], ry_send.at[d], ry_recv.at[d], at(t, z, c, h))

    def rz_copy(d):
        t = (z + d) % Z
        return rcopy(prom_y.at[0, t], prom_z.at[d], rz_send.at[d], rz_recv.at[d], at(y, t, c, h))

    def grad_body(b, carry):
        values = kvb[b, 1]
        kt = kvt[b, 0]
        for n in range(NC):
            cols = slice(n * CB, (n + 1) * CB)
            dp = dot_nn(values, dot_t[:, cols])
            w = p_scr[b, :, cols].astype(F32) * inv[:, cols]
            ds = (w * (dp - delta[:, cols])).astype(BF)
            dv = dot_nn(w.astype(BF), dor[cols, :])
            dk = dot_nn(ds, qr[cols, :])
            dq_acc[:, cols] += dot_nn(kt, ds)
            if n == 0:
                acc[0] = dk
                acc[1] = dv
            else:
                acc[0] += dk
                acc[1] += dv

        per_y = Z * 2

        for blk in range(NPB):

            @pl.when(b == blk)
            def _():
                for i in range(KB // U):
                    s = blk * (KB // U) + i
                    rows = slice(i * U, (i + 1) * U)
                    both = jnp.concatenate([acc[0, rows, :] * scale, acc[1, rows, :]], axis=0)
                    prom_s[s % 2, s // per_y, (s // 2) % Z] = both.astype(BF)

            @pl.when(b == blk)
            def _():
                rc_copy(blk).start()

        @pl.when(b >= NPB)
        def _():
            p = b - NPB
            for half in range(2):
                rows = slice(half * T, (half + 1) * T)
                xs[p, half, 0] = (acc[0, rows, :] * scale).astype(BF)
                xs[p, half, 1] = acc[1, rows, :].astype(BF)
            gx_copy(p).start()

        for k in range(NPB):

            @pl.when(b == k + 1)
            def _():
                rc_copy(k).wait()
                ys = slice(k * YB, (k + 1) * YB)
                prom_s[c, ys] = (prom_s[c, ys].astype(F32) + prom_r[ys].astype(F32)).astype(BF)
                for d in range(1, Y):
                    t = (y + d) % Y

                    @pl.when(t // YB == k)
                    def _():
                        ry_copy(d).start()

        @pl.when(b > NPB)
        def _():
            p = b - NPB - 1
            gx_copy(p).wait()
            zs[p] = (xs[p, c].astype(F32) + xr[p].astype(F32)).astype(BF)
            gz_copy(p).start()

        return carry

    lax.fori_loop(0, nb, grad_body, 0)

    total = prom_s[c, y].astype(F32)
    for d in range(1, Y):
        ry_copy(d).wait_recv()
        total += prom_y[d].astype(F32)
    prom_y[0] = total.astype(BF)
    for d in range(1, Z):
        rz_copy(d).start()

    for g in range(G):
        rows = slice(g * T, (g + 1) * T)
        dq_v[:, g * W : (g + 1) * W] = (dq_acc[:, rows] * scale).T.astype(BF)
    dq_out = pltpu.make_async_copy(dq_v, dq_ref, out_sem.at[1])
    dq_out.start()

    gx_copy(z).wait()
    mine = xs[z, c].astype(F32) + xr[z].astype(F32)
    acc2 = acc
    acc2[0, :T] = mine[0]
    acc2[1, :T] = mine[1]
    for d in range(1, Z):

        @pl.when(z + d < Z)
        def _():
            gz_from(d).wait_recv()
            acc2[0, :T] += zr[d, 0].astype(F32)
            acc2[1, :T] += zr[d, 1].astype(F32)

    dk_v[...] = acc2[0, :T].astype(BF)
    dv_v[...] = acc2[1, :T].astype(BF)
    dk_out = pltpu.make_async_copy(dk_v, dk_ref, out_sem.at[2])
    dv_out = pltpu.make_async_copy(dv_v, dv_ref, out_sem.at[3])
    dk_out.start()
    dv_out.start()

    last = prom_y[0, z].astype(F32)
    for d in range(1, Z):
        rz_copy(d).wait_recv()
        last += prom_z[d].astype(F32)
    pdk_v[...] = last[:U]
    pdv_v[...] = last[U:]
    pdk_out = pltpu.make_async_copy(pdk_v, pdk_ref, out_sem.at[4])
    pdv_out = pltpu.make_async_copy(pdv_v, pdv_ref, out_sem.at[5])
    pdk_out.start()
    pdv_out.start()
    for copy in (att_out, dq_out, dk_out, dv_out, pdk_out, pdv_out):
        copy.wait()

    for a in range(3):
        for d in range(1, H):
            a2a_copy(a, d).wait_send()
    for d in range(1, Z):
        pz_copy(d).wait_send()
        rz_copy(d).wait_send()
    for d in range(1, Y):
        py_copy(d).wait_send()
        ry_copy(d).wait_send()
    pc_copy(c).wait_send()
    for d in range(1, Z):

        @pl.when(z + d < Z)
        def _():
            kz_copy(d).wait_send()

        @pl.when(z - d >= 0)
        def _():
            kc_copy(d).wait_send()
            gz_copy(z - d).wait_send()


def write_out(*refs):
    given, written, held, sems = refs[:6], refs[6:12], refs[12:18], refs[18]
    reads = [pltpu.make_async_copy(given[i], held[i], sems.at[0, i]) for i in range(6)]
    writes = [pltpu.make_async_copy(held[i], written[i], sems.at[1, i]) for i in range(6)]
    for copy in reads:
        copy.start()
    for i in range(6):
        reads[i].wait()
        writes[i].start()
    for copy in writes:
        copy.wait()


def solution(mesh):
    H = mesh.shape["head"]
    S = mesh.shape["seq"]

    def per_device(q, rk, rv, pk, pv, do, lengths):
        TR = q.shape[0]
        T = TR * H
        Y = lengths.shape[0]
        Z = S // Y // 2
        U = pk.shape[0]
        R = T * G
        NB = U * S // KB + Z
        dims = (H, Y, Z, TR, U)
        dma = pltpu.SemaphoreType.DMA
        vm = pltpu.VMEM
        any_spec = pl.BlockSpec(memory_space=pl.ANY)
        shapes = [
            jax.ShapeDtypeStruct((T, G * W), BF),
            jax.ShapeDtypeStruct((T, G * W), BF),
            jax.ShapeDtypeStruct((T, W), BF),
            jax.ShapeDtypeStruct((T, W), BF),
            jax.ShapeDtypeStruct((U, W), F32),
            jax.ShapeDtypeStruct((U, W), F32),
        ]
        results = pl.pallas_call(
            functools.partial(kernel, dims),
            out_shape=shapes,
            in_specs=[any_spec] * 7,
            out_specs=[any_spec] * 6,
            scratch_shapes=[
                vm((U, W), BF),
                vm((U, W), BF),
                pltpu.SMEM((Y,), jnp.int32),
                vm((2, TR, H * W), BF),
                dma((5,)),
                dma((6,)),
            ]
            + [vm(x.shape, x.dtype) for x in shapes]
            + [
                vm((T, G * W), BF),
                vm((T, G * W), BF),
                vm((NB, 2, KB, W), BF),
                vm((NB, 2, W, KB), BF),
                vm((2, Y, Z, 2 * U, W), BF),
                vm((R, W), BF),
                vm((R, W), BF),
                vm((W, R), BF),
                vm((NB, KB, R), F32),
                vm((NB, KB, R), BF),
                vm((8, R), F32),
                vm((8, R), F32),
                vm((W, R), F32),
                vm((W, R), F32),
                vm((2, KB, W), F32),
                vm((2, Y, Z, 2 * U, W), BF),
                vm((Y, Z, 2 * U, W), BF),
                vm((Y, Z, 2 * U, W), BF),
                vm((Z, 2 * U, W), BF),
                vm((Z, 2, 2, T, W), BF),
                vm((Z, 2, T, W), BF),
                vm((Z, 2, T, W), BF),
                vm((Z, 2, T, W), BF),
                dma((3, H)),
                dma((3, H)),
                dma((3,)),
                dma((Z,)),
                dma((Z,)),
                dma((Y,)),
                dma((Y,)),
                dma,
                dma,
                dma((Z,)),
                dma((Z,)),
                dma((Z,)),
                dma((Z,)),
                dma((Z,)),
                dma((Z,)),
                dma((Z,)),
                dma((Z,)),
                dma((U * S // KB,)),
                dma((U * S // KB,)),
                dma((Y,)),
                dma((Y,)),
                dma((Z,)),
                dma((Z,)),
            ],
            compiler_params=pltpu.CompilerParams(
                collective_id=0, has_side_effects=True, vmem_limit_bytes=60 * 1024 * 1024
            ),
        )(q, rk, rv, pk, pv, do, lengths)
        return pl.pallas_call(
            write_out,
            out_shape=shapes,
            in_specs=[any_spec] * 6,
            out_specs=[any_spec] * 6,
            scratch_shapes=[vm(x.shape, x.dtype) for x in shapes] + [dma((2, 6))],
            compiler_params=pltpu.CompilerParams(vmem_limit_bytes=60 * 1024 * 1024),
        )(*results)

    tok = P(("seq", "head"), None)
    par = P("seq", "head")
    return jax.shard_map(
        per_device,
        mesh=mesh,
        in_specs=(tok, tok, tok, par, par, tok, P()),
        out_specs=(par,) * 6,
        check_vma=False,
    )
```

```python
import functools
import math

import jax
import jax.numpy as jnp
from jax import lax
from jax.experimental import pallas as pl
from jax.experimental.pallas import tpu as pltpu
from jax.sharding import PartitionSpec as P

MESH = pl.DeviceIdType.MESH
BF = jnp.bfloat16
F32 = jnp.float32
W = 128
G = 8
KB = 256
CB = 512
NEG = -1e30


def dot_nt(a, b):
    return lax.dot_general(a, b, (((1,), (1,)), ((), ())), preferred_element_type=F32)


def dot_nn(a, b):
    return lax.dot_general(a, b, (((1,), (0,)), ((), ())), preferred_element_type=F32)


def kernel(
    dims,
    q_hbm,
    k_hbm,
    v_hbm,
    pk_hbm,
    pv_hbm,
    do_hbm,
    len_hbm,
    att_ref,
    dq_ref,
    dk_ref,
    dv_ref,
    pdk_ref,
    pdv_ref,
    pk_ref,
    pv_ref,
    len_ref,
    kv_held,
    small_sem,
    out_sem,
    att_v,
    dq_v,
    dk_v,
    dv_v,
    pdk_v,
    pdv_v,
    q_all,
    do_all,
    kvb,
    kvt,
    pg,
    qr,
    dor,
    dot_t,
    s_scr,
    p_scr,
    mx,
    lx,
    o_acc,
    dq_acc,
    acc,
    prom_s,
    prom_r,
    prom_y,
    prom_z,
    xs,
    xr,
    zs,
    zr,
    a2a_send,
    a2a_recv,
    own_sem,
    pz_send,
    pz_recv,
    py_send,
    py_recv,
    pc_send,
    pc_recv,
    kz_send,
    kz_recv,
    kc_send,
    kc_recv,
    gx_send,
    gx_recv,
    gz_send,
    gz_recv,
    rc_send,
    rc_recv,
    ry_send,
    ry_recv,
    rz_send,
    rz_recv,
):
    H, Y, Z, TR, U = dims
    T = H * TR
    R = T * G
    PT = U * Y * Z * 2
    NPB = PT // KB
    NC = R // CB
    GC = CB // T
    scale = W**-0.5
    c2 = scale * math.log2(math.e)

    s_me = lax.axis_index("seq")
    h = lax.axis_index("head")
    c = s_me % 2
    z = (s_me // 2) % Z
    y = s_me // (2 * Z)

    def at(yy, zz, cc, hh):
        return {"seq": (yy * Z + zz) * 2 + cc, "head": hh}

    def rcopy(src, dst, ssem, rsem, dev):
        return pltpu.make_async_remote_copy(
            src_ref=src, dst_ref=dst, send_sem=ssem, recv_sem=rsem, device_id=dev, device_id_type=MESH
        )

    other = at(y, z, 1 - c, h)

    small = [
        pltpu.make_async_copy(pk_hbm, pk_ref, small_sem.at[0]),
        pltpu.make_async_copy(pv_hbm, pv_ref, small_sem.at[1]),
        pltpu.make_async_copy(len_hbm, len_ref, small_sem.at[2]),
        pltpu.make_async_copy(k_hbm, kv_held.at[0], small_sem.at[3]),
        pltpu.make_async_copy(v_hbm, kv_held.at[1], small_sem.at[4]),
    ]
    for copy in small:
        copy.start()

    barrier = pltpu.get_barrier_semaphore()
    for d in range(1, H):
        pl.semaphore_signal(barrier, inc=1, device_id=at(y, z, c, (h + d) % H), device_id_type=MESH)
    for d in range(1, Y):
        pl.semaphore_signal(barrier, inc=1, device_id=at((y + d) % Y, z, c, h), device_id_type=MESH)
    for d in range(1, Z):
        pl.semaphore_signal(barrier, inc=1, device_id=at(y, (z + d) % Z, c, h), device_id_type=MESH)
    pl.semaphore_signal(barrier, inc=1, device_id=other, device_id_type=MESH)
    pl.semaphore_wait(barrier, H + Y + Z - 2)

    my_blk = NPB + z
    my_rows = pl.multiple_of(c * T, T)
    GW = G * W

    def src_dst(a, t, rows):
        row = pl.ds(pl.multiple_of(rows * TR, TR), TR)
        kv_row = pl.ds(pl.multiple_of(c * T + rows * TR, TR), TR)
        wide = pl.ds(pl.multiple_of(t * GW, GW), GW)
        thin = pl.ds(pl.multiple_of(t * W, W), W)
        if a == 0:
            return kv_held.at[:, :, thin], kvb.at[my_blk, :, kv_row, :]
        if a == 1:
            return q_hbm.at[:, wide], q_all.at[row, :]
        return do_hbm.at[:, wide], do_all.at[row, :]

    def a2a_copy(a, d):
        t = (h + d) % H
        src, dst = src_dst(a, t, h)
        return rcopy(src, dst, a2a_send.at[a, d], a2a_recv.at[a, d], at(y, z, c, t))

    def own_copy(a):
        src, dst = src_dst(a, h, h)
        return pltpu.make_async_copy(src, dst, own_sem.at[a])

    def a2a_start(a):
        own_copy(a).start()
        for d in range(1, H):
            a2a_copy(a, d).start()

    def a2a_wait(a):
        own_copy(a).wait()
        for d in range(1, H):
            frm = (h + H - d) % H
            src, dst = src_dst(a, h, frm)
            rcopy(src, dst, a2a_send.at[a, d], a2a_recv.at[a, d], at(y, z, c, frm)).wait_recv()

    for copy in small:
        copy.wait()
    unit = jnp.concatenate([pk_ref[...].astype(F32), pv_ref[...].astype(F32)], axis=0)
    pg[c, y, z] = unit.astype(BF)

    def pz_copy(d):
        return rcopy(
            pg.at[c, y, z], pg.at[c, y, z], pz_send.at[d], pz_recv.at[d], at(y, (z + d) % Z, c, h)
        )

    def pz_from(d):
        f = (z + Z - d) % Z
        return rcopy(pg.at[c, y, f], pg.at[c, y, f], pz_send.at[d], pz_recv.at[d], at(y, f, c, h))

    for d in range(1, Z):
        pz_copy(d).start()
    a2a_start(0)
    a2a_start(1)

    def py_copy(d):
        return rcopy(pg.at[c, y], pg.at[c, y], py_send.at[d], py_recv.at[d], at((y + d) % Y, z, c, h))

    def py_from(d):
        f = (y + Y - d) % Y
        return rcopy(pg.at[c, f], pg.at[c, f], py_send.at[d], py_recv.at[d], at(f, z, c, h))

    def span_ref(zz, cc):
        return kvb.at[NPB + zz, :, pl.ds(pl.multiple_of(cc * T, T), T), :]

    def kz_copy(d):
        return rcopy(
            span_ref(z, c), span_ref(z, c), kz_send.at[d], kz_recv.at[d], at(y, z + d, c, h)
        )

    def kz_from(d):
        return rcopy(
            span_ref(z - d, c), span_ref(z - d, c), kz_send.at[d], kz_recv.at[d], at(y, z - d, c, h)
        )

    def kc_copy(d):
        return rcopy(span_ref(z - d, c), span_ref(z - d, c), kc_send.at[d], kc_recv.at[d], other)

    def kc_from(d):
        return rcopy(
            span_ref(z - d, 1 - c), span_ref(z - d, 1 - c), kc_send.at[d], kc_recv.at[d], other
        )

    def pc_copy(cc):
        return rcopy(pg.at[cc], pg.at[cc], pc_send, pc_recv, other)

    a2a_wait(0)
    for d in range(Z - 1, 0, -1):

        @pl.when(z + d < Z)
        def _():
            kz_copy(d).start()

    kc_copy(0).start()
    for d in range(1, Z):
        pz_from(d).wait_recv()
    for d in range(1, Y):
        py_copy(d).start()
    a2a_start(2)

    nb = NPB + z + 1
    mx[...] = jnp.full_like(mx, NEG)

    def scores(b, edge):
        rel = lax.broadcasted_iota(jnp.int32, (KB, T), 0) - lax.broadcasted_iota(jnp.int32, (KB, T), 1)
        seen = jnp.concatenate([rel <= c * T] * GC, axis=1)
        keys = kvb[b, 0]
        kvt[b, 0] = keys.T
        kvt[b, 1] = kvb[b, 1].T
        for n in range(NC):
            cols = slice(n * CB, (n + 1) * CB)
            s = dot_nt(keys, qr[cols, :])
            if edge:
                s = jnp.where(seen, s, NEG)
            s_scr[b, :, cols] = s
            mx[:, cols] = jnp.maximum(mx[:, cols], jnp.max(s.reshape(KB // 8, 8, CB), axis=0))

    def score_body(b, carry):
        scores(b, False)
        return carry

    a2a_wait(1)
    for g in range(G):
        qr[g * T : (g + 1) * T, :] = q_all[:, g * W : (g + 1) * W]
    for d in range(1, Y):
        py_from(d).wait_recv()
    pc_copy(c).start()
    for d in range(1, Z):

        @pl.when(z - d >= 0)
        def _():
            kz_from(d).wait_recv()
            kc_copy(d).start()

    pc_copy(1 - c).wait_recv()
    units = []
    for s in range(Y * Z * 2):
        units.append(pg[s % 2, s // (2 * Z), (s // 2) % Z].astype(F32))
    per = KB // U
    for b in range(NPB):
        part = units[b * per : (b + 1) * per]
        kvb[b, 0] = jnp.concatenate([u[:U] for u in part], axis=0).astype(BF)
        kvb[b, 1] = jnp.concatenate([u[U:] for u in part], axis=0).astype(BF)

    kc_copy(0).wait_send()
    kc_from(0).wait_recv()
    scores(nb - 1, True)
    lax.fori_loop(0, NPB, score_body, 0)
    for d in range(1, Z):

        @pl.when(z - d >= 0)
        def _():
            kc_from(d).wait_recv()

    lax.fori_loop(NPB, nb - 1, score_body, 0)
    top = jnp.max(mx[...], axis=0, keepdims=True) * c2
    lx[...] = jnp.zeros_like(lx)
    o_acc[...] = jnp.zeros_like(o_acc)

    def weight_body(b, carry):
        vt = kvt[b, 1]
        for n in range(NC):
            cols = slice(n * CB, (n + 1) * CB)
            e = jnp.exp2(s_scr[b, :, cols] * c2 - top[:, cols])
            lx[:, cols] += jnp.sum(e.reshape(KB // 8, 8, CB), axis=0)
            p = e.astype(BF)
            p_scr[b, :, cols] = p
            o_acc[:, cols] += dot_nn(vt, p)
        return carry

    lax.fori_loop(0, nb, weight_body, 0)
    inv = 1.0 / jnp.sum(lx[...], axis=0, keepdims=True)

    length = len_ref[y]
    first = (2 * z + c) * T
    live_col = first + lax.broadcasted_iota(jnp.int32, (W, T), 1) < length
    live_row = first + lax.broadcasted_iota(jnp.int32, (T, W), 0) < length

    for g in range(G):
        rows = slice(g * T, (g + 1) * T)
        out_t = jnp.where(live_col, o_acc[:, rows] * inv[:, rows], 0.0)
        att_v[:, g * W : (g + 1) * W] = out_t.T.astype(BF)
        o_acc[:, rows] = out_t.astype(BF).astype(F32)
    att_out = pltpu.make_async_copy(att_v, att_ref, out_sem.at[0])
    att_out.start()

    a2a_wait(2)
    deltas = []
    for g in range(G):
        rows = slice(g * T, (g + 1) * T)
        grad = jnp.where(live_row, do_all[:, g * W : (g + 1) * W].astype(F32), 0.0)
        dor[rows, :] = grad.astype(BF)
        grad_t = grad.T
        dot_t[:, rows] = grad_t.astype(BF)
        deltas.append(jnp.sum(grad_t * o_acc[:, rows], axis=0, keepdims=True))
    delta = jnp.concatenate(deltas, axis=1)
    dq_acc[...] = jnp.zeros_like(dq_acc)

    def gx_copy(p):
        return rcopy(xs.at[p, 1 - c], xr.at[p], gx_send.at[p], gx_recv.at[p], other)

    def gz_copy(p):
        return rcopy(zs.at[p], zr.at[z - p], gz_send.at[p], gz_recv.at[z - p], at(y, p, c, h))

    def gz_from(d):
        return rcopy(zs.at[z], zr.at[d], gz_send.at[z], gz_recv.at[d], at(y, z + d, c, h))

    YB = Y // NPB

    def rc_copy(k):
        ys = pl.ds(k * YB, YB)
        return rcopy(prom_s.at[1 - c, ys], prom_r.at[ys], rc_send.at[k], rc_recv.at[k], other)

    def ry_copy(d):
        t = (y + d) % Y
        return rcopy(prom_s.at[c, t], prom_y.at[d], ry_send.at[d], ry_recv.at[d], at(t, z, c, h))

    def rz_copy(d):
        t = (z + d) % Z
        return rcopy(prom_y.at[0, t], prom_z.at[d], rz_send.at[d], rz_recv.at[d], at(y, t, c, h))

    def grad_body(b, carry):
        values = kvb[b, 1]
        kt = kvt[b, 0]
        for n in range(NC):
            cols = slice(n * CB, (n + 1) * CB)
            dp = dot_nn(values, dot_t[:, cols])
            w = p_scr[b, :, cols].astype(F32) * inv[:, cols]
            ds = (w * (dp - delta[:, cols])).astype(BF)
            dv = dot_nn(w.astype(BF), dor[cols, :])
            dk = dot_nn(ds, qr[cols, :])
            dq_acc[:, cols] += dot_nn(kt, ds)
            if n == 0:
                acc[0] = dk
                acc[1] = dv
            else:
                acc[0] += dk
                acc[1] += dv

        per_y = Z * 2

        for blk in range(NPB):

            @pl.when(b == blk)
            def _():
                for i in range(KB // U):
                    s = blk * (KB // U) + i
                    rows = slice(i * U, (i + 1) * U)
                    both = jnp.concatenate([acc[0, rows, :] * scale, acc[1, rows, :]], axis=0)
                    prom_s[s % 2, s // per_y, (s // 2) % Z] = both.astype(BF)

            @pl.when(b == blk)
            def _():
                rc_copy(blk).start()

        @pl.when(b >= NPB)
        def _():
            p = b - NPB
            for half in range(2):
                rows = slice(half * T, (half + 1) * T)
                xs[p, half, 0] = (acc[0, rows, :] * scale).astype(BF)
                xs[p, half, 1] = acc[1, rows, :].astype(BF)
            gx_copy(p).start()

        for k in range(NPB):

            @pl.when(b == k + 1)
            def _():
                rc_copy(k).wait()
                ys = slice(k * YB, (k + 1) * YB)
                prom_s[c, ys] = (prom_s[c, ys].astype(F32) + prom_r[ys].astype(F32)).astype(BF)
                for d in range(1, Y):
                    t = (y + d) % Y

                    @pl.when(t // YB == k)
                    def _():
                        ry_copy(d).start()

        @pl.when(b > NPB)
        def _():
            p = b - NPB - 1
            gx_copy(p).wait()
            zs[p] = (xs[p, c].astype(F32) + xr[p].astype(F32)).astype(BF)
            gz_copy(p).start()

        return carry

    lax.fori_loop(0, nb, grad_body, 0)

    total = prom_s[c, y].astype(F32)
    for d in range(1, Y):
        ry_copy(d).wait_recv()
        total += prom_y[d].astype(F32)
    prom_y[0] = total.astype(BF)
    for d in range(1, Z):
        rz_copy(d).start()

    for g in range(G):
        rows = slice(g * T, (g + 1) * T)
        dq_v[:, g * W : (g + 1) * W] = (dq_acc[:, rows] * scale).T.astype(BF)
    dq_out = pltpu.make_async_copy(dq_v, dq_ref, out_sem.at[1])
    dq_out.start()

    gx_copy(z).wait()
    mine = xs[z, c].astype(F32) + xr[z].astype(F32)
    acc2 = acc
    acc2[0, :T] = mine[0]
    acc2[1, :T] = mine[1]
    for d in range(1, Z):

        @pl.when(z + d < Z)
        def _():
            gz_from(d).wait_recv()
            acc2[0, :T] += zr[d, 0].astype(F32)
            acc2[1, :T] += zr[d, 1].astype(F32)

    dk_v[...] = acc2[0, :T].astype(BF)
    dv_v[...] = acc2[1, :T].astype(BF)
    dk_out = pltpu.make_async_copy(dk_v, dk_ref, out_sem.at[2])
    dv_out = pltpu.make_async_copy(dv_v, dv_ref, out_sem.at[3])
    dk_out.start()
    dv_out.start()

    last = prom_y[0, z].astype(F32)
    for d in range(1, Z):
        rz_copy(d).wait_recv()
        last += prom_z[d].astype(F32)
    pdk_v[...] = last[:U]
    pdv_v[...] = last[U:]
    pdk_out = pltpu.make_async_copy(pdk_v, pdk_ref, out_sem.at[4])
    pdv_out = pltpu.make_async_copy(pdv_v, pdv_ref, out_sem.at[5])
    pdk_out.start()
    pdv_out.start()
    for copy in (att_out, dq_out, dk_out, dv_out, pdk_out, pdv_out):
        copy.wait()

    for a in range(3):
        for d in range(1, H):
            a2a_copy(a, d).wait_send()
    for d in range(1, Z):
        pz_copy(d).wait_send()
        rz_copy(d).wait_send()
    for d in range(1, Y):
        py_copy(d).wait_send()
        ry_copy(d).wait_send()
    pc_copy(c).wait_send()
    for d in range(1, Z):

        @pl.when(z + d < Z)
        def _():
            kz_copy(d).wait_send()

        @pl.when(z - d >= 0)
        def _():
            kc_copy(d).wait_send()
            gz_copy(z - d).wait_send()


def write_out(*refs):
    given, written, held, sems = refs[:6], refs[6:12], refs[12:18], refs[18]
    reads = [pltpu.make_async_copy(given[i], held[i], sems.at[0, i]) for i in range(6)]
    writes = [pltpu.make_async_copy(held[i], written[i], sems.at[1, i]) for i in range(6)]
    for copy in reads:
        copy.start()
    for i in range(6):
        reads[i].wait()
        writes[i].start()
    for copy in writes:
        copy.wait()


def solution(mesh):
    H = mesh.shape["head"]
    S = mesh.shape["seq"]

    def per_device(q, rk, rv, pk, pv, do, lengths):
        TR = q.shape[0]
        T = TR * H
        Y = lengths.shape[0]
        Z = S // Y // 2
        U = pk.shape[0]
        R = T * G
        NB = U * S // KB + Z
        dims = (H, Y, Z, TR, U)
        dma = pltpu.SemaphoreType.DMA
        vm = pltpu.VMEM
        any_spec = pl.BlockSpec(memory_space=pl.ANY)
        shapes = [
            jax.ShapeDtypeStruct((T, G * W), BF),
            jax.ShapeDtypeStruct((T, G * W), BF),
            jax.ShapeDtypeStruct((T, W), BF),
            jax.ShapeDtypeStruct((T, W), BF),
            jax.ShapeDtypeStruct((U, W), F32),
            jax.ShapeDtypeStruct((U, W), F32),
        ]
        results = pl.pallas_call(
            functools.partial(kernel, dims),
            out_shape=shapes,
            in_specs=[any_spec] * 7,
            out_specs=[any_spec] * 6,
            scratch_shapes=[
                vm((U, W), BF),
                vm((U, W), BF),
                pltpu.SMEM((Y,), jnp.int32),
                vm((2, TR, H * W), BF),
                dma((5,)),
                dma((6,)),
            ]
            + [vm(x.shape, x.dtype) for x in shapes]
            + [
                vm((T, G * W), BF),
                vm((T, G * W), BF),
                vm((NB, 2, KB, W), BF),
                vm((NB, 2, W, KB), BF),
                vm((2, Y, Z, 2 * U, W), BF),
                vm((R, W), BF),
                vm((R, W), BF),
                vm((W, R), BF),
                vm((NB, KB, R), F32),
                vm((NB, KB, R), BF),
                vm((8, R), F32),
                vm((8, R), F32),
                vm((W, R), F32),
                vm((W, R), F32),
                vm((2, KB, W), F32),
                vm((2, Y, Z, 2 * U, W), BF),
                vm((Y, Z, 2 * U, W), BF),
                vm((Y, Z, 2 * U, W), BF),
                vm((Z, 2 * U, W), BF),
                vm((Z, 2, 2, T, W), BF),
                vm((Z, 2, T, W), BF),
                vm((Z, 2, T, W), BF),
                vm((Z, 2, T, W), BF),
                dma((3, H)),
                dma((3, H)),
                dma((3,)),
                dma((Z,)),
                dma((Z,)),
                dma((Y,)),
                dma((Y,)),
                dma,
                dma,
                dma((Z,)),
                dma((Z,)),
                dma((Z,)),
                dma((Z,)),
                dma((Z,)),
                dma((Z,)),
                dma((Z,)),
                dma((Z,)),
                dma((U * S // KB,)),
                dma((U * S // KB,)),
                dma((Y,)),
                dma((Y,)),
                dma((Z,)),
                dma((Z,)),
            ],
            compiler_params=pltpu.CompilerParams(
                collective_id=0, has_side_effects=True, vmem_limit_bytes=60 * 1024 * 1024
            ),
        )(q, rk, rv, pk, pv, do, lengths)
        return pl.pallas_call(
            write_out,
            out_shape=shapes,
            in_specs=[any_spec] * 6,
            out_specs=[any_spec] * 6,
            scratch_shapes=[vm(x.shape, x.dtype) for x in shapes] + [dma((2, 6))],
            compiler_params=pltpu.CompilerParams(vmem_limit_bytes=60 * 1024 * 1024),
        )(*results)

    tok = P(("seq", "head"), None)
    par = P("seq", "head")
    return jax.shard_map(
        per_device,
        mesh=mesh,
        in_specs=(tok, tok, tok, par, par, tok, P()),
        out_specs=(par,) * 6,
        check_vma=False,
    )
```

```python
import functools
import math

import jax
import jax.numpy as jnp
from jax import lax
from jax.experimental import pallas as pl
from jax.experimental.pallas import tpu as pltpu
from jax.sharding import PartitionSpec as P

MESH = pl.DeviceIdType.MESH
BF = jnp.bfloat16
F32 = jnp.float32
W = 128
G = 8
KB = 256
CB = 512
NEG = -1e30


def dot_nt(a, b):
    return lax.dot_general(a, b, (((1,), (1,)), ((), ())), preferred_element_type=F32)


def dot_nn(a, b):
    return lax.dot_general(a, b, (((1,), (0,)), ((), ())), preferred_element_type=F32)


def kernel(
    dims,
    q_hbm,
    k_hbm,
    v_hbm,
    pk_hbm,
    pv_hbm,
    do_hbm,
    len_hbm,
    att_ref,
    dq_ref,
    dk_ref,
    dv_ref,
    pdk_ref,
    pdv_ref,
    pk_ref,
    pv_ref,
    len_ref,
    kv_held,
    small_sem,
    out_sem,
    att_v,
    dq_v,
    dk_v,
    dv_v,
    pdk_v,
    pdv_v,
    q_all,
    do_all,
    kvb,
    kvt,
    pg,
    qr,
    dor,
    dot_t,
    s_scr,
    p_scr,
    mx,
    lx,
    o_acc,
    dq_acc,
    acc,
    prom_s,
    prom_r,
    prom_y,
    prom_z,
    xs,
    xr,
    zs,
    zr,
    a2a_send,
    a2a_recv,
    own_sem,
    pz_send,
    pz_recv,
    py_send,
    py_recv,
    pc_send,
    pc_recv,
    kz_send,
    kz_recv,
    kc_send,
    kc_recv,
    gx_send,
    gx_recv,
    gz_send,
    gz_recv,
    rc_send,
    rc_recv,
    ry_send,
    ry_recv,
    rz_send,
    rz_recv,
):
    H, Y, Z, TR, U = dims
    T = H * TR
    R = T * G
    PT = U * Y * Z * 2
    NPB = PT // KB
    NC = R // CB
    GC = CB // T
    scale = W**-0.5
    c2 = scale * math.log2(math.e)

    s_me = lax.axis_index("seq")
    h = lax.axis_index("head")
    c = s_me % 2
    z = (s_me // 2) % Z
    y = s_me // (2 * Z)

    def at(yy, zz, cc, hh):
        return {"seq": (yy * Z + zz) * 2 + cc, "head": hh}

    def rcopy(src, dst, ssem, rsem, dev):
        return pltpu.make_async_remote_copy(
            src_ref=src, dst_ref=dst, send_sem=ssem, recv_sem=rsem, device_id=dev, device_id_type=MESH
        )

    other = at(y, z, 1 - c, h)

    small = [
        pltpu.make_async_copy(pk_hbm, pk_ref, small_sem.at[0]),
        pltpu.make_async_copy(pv_hbm, pv_ref, small_sem.at[1]),
        pltpu.make_async_copy(len_hbm, len_ref, small_sem.at[2]),
        pltpu.make_async_copy(k_hbm, kv_held.at[0], small_sem.at[3]),
        pltpu.make_async_copy(v_hbm, kv_held.at[1], small_sem.at[4]),
    ]
    for copy in small:
        copy.start()

    barrier = pltpu.get_barrier_semaphore()
    for d in range(1, H):
        pl.semaphore_signal(barrier, inc=1, device_id=at(y, z, c, (h + d) % H), device_id_type=MESH)
    for d in range(1, Y):
        pl.semaphore_signal(barrier, inc=1, device_id=at((y + d) % Y, z, c, h), device_id_type=MESH)
    for d in range(1, Z):
        pl.semaphore_signal(barrier, inc=1, device_id=at(y, (z + d) % Z, c, h), device_id_type=MESH)
    pl.semaphore_signal(barrier, inc=1, device_id=other, device_id_type=MESH)
    pl.semaphore_wait(barrier, H + Y + Z - 2)

    my_blk = NPB + z
    my_rows = pl.multiple_of(c * T, T)
    GW = G * W

    def src_dst(a, t, rows):
        row = pl.ds(pl.multiple_of(rows * TR, TR), TR)
        kv_row = pl.ds(pl.multiple_of(c * T + rows * TR, TR), TR)
        wide = pl.ds(pl.multiple_of(t * GW, GW), GW)
        thin = pl.ds(pl.multiple_of(t * W, W), W)
        if a == 0:
            return kv_held.at[:, :, thin], kvb.at[my_blk, :, kv_row, :]
        if a == 1:
            return q_hbm.at[:, wide], q_all.at[row, :]
        return do_hbm.at[:, wide], do_all.at[row, :]

    def a2a_copy(a, d):
        t = (h + d) % H
        src, dst = src_dst(a, t, h)
        return rcopy(src, dst, a2a_send.at[a, d], a2a_recv.at[a, d], at(y, z, c, t))

    def own_copy(a):
        src, dst = src_dst(a, h, h)
        return pltpu.make_async_copy(src, dst, own_sem.at[a])

    def a2a_start(a):
        own_copy(a).start()
        for d in range(1, H):
            a2a_copy(a, d).start()

    def a2a_wait(a):
        own_copy(a).wait()
        for d in range(1, H):
            frm = (h + H - d) % H
            src, dst = src_dst(a, h, frm)
            rcopy(src, dst, a2a_send.at[a, d], a2a_recv.at[a, d], at(y, z, c, frm)).wait_recv()

    for copy in small:
        copy.wait()
    unit = jnp.concatenate([pk_ref[...].astype(F32), pv_ref[...].astype(F32)], axis=0)
    pg[c, y, z] = unit.astype(BF)

    def pz_copy(d):
        return rcopy(
            pg.at[c, y, z], pg.at[c, y, z], pz_send.at[d], pz_recv.at[d], at(y, (z + d) % Z, c, h)
        )

    def pz_from(d):
        f = (z + Z - d) % Z
        return rcopy(pg.at[c, y, f], pg.at[c, y, f], pz_send.at[d], pz_recv.at[d], at(y, f, c, h))

    for d in range(1, Z):
        pz_copy(d).start()
    a2a_start(0)
    a2a_start(1)

    def py_copy(d):
        return rcopy(pg.at[c, y], pg.at[c, y], py_send.at[d], py_recv.at[d], at((y + d) % Y, z, c, h))

    def py_from(d):
        f = (y + Y - d) % Y
        return rcopy(pg.at[c, f], pg.at[c, f], py_send.at[d], py_recv.at[d], at(f, z, c, h))

    def span_ref(zz, cc):
        return kvb.at[NPB + zz, :, pl.ds(pl.multiple_of(cc * T, T), T), :]

    def kz_copy(d):
        return rcopy(
            span_ref(z, c), span_ref(z, c), kz_send.at[d], kz_recv.at[d], at(y, z + d, c, h)
        )

    def kz_from(d):
        return rcopy(
            span_ref(z - d, c), span_ref(z - d, c), kz_send.at[d], kz_recv.at[d], at(y, z - d, c, h)
        )

    def kc_copy(d):
        return rcopy(span_ref(z - d, c), span_ref(z - d, c), kc_send.at[d], kc_recv.at[d], other)

    def kc_from(d):
        return rcopy(
            span_ref(z - d, 1 - c), span_ref(z - d, 1 - c), kc_send.at[d], kc_recv.at[d], other
        )

    def pc_copy(cc):
        return rcopy(pg.at[cc], pg.at[cc], pc_send, pc_recv, other)

    a2a_wait(0)
    for d in range(Z - 1, 0, -1):

        @pl.when(z + d < Z)
        def _():
            kz_copy(d).start()

    kc_copy(0).start()
    for d in range(1, Z):
        pz_from(d).wait_recv()
    for d in range(1, Y):
        py_copy(d).start()
    a2a_start(2)

    nb = NPB + z + 1
    mx[...] = jnp.full_like(mx, NEG)

    def scores(b, edge):
        rel = lax.broadcasted_iota(jnp.int32, (KB, T), 0) - lax.broadcasted_iota(jnp.int32, (KB, T), 1)
        seen = jnp.concatenate([rel <= c * T] * GC, axis=1)
        keys = kvb[b, 0]
        kvt[b, 0] = keys.T
        kvt[b, 1] = kvb[b, 1].T
        for n in range(NC):
            cols = slice(n * CB, (n + 1) * CB)
            s = dot_nt(keys, qr[cols, :])
            if edge:
                s = jnp.where(seen, s, NEG)
            s_scr[b, :, cols] = s
            mx[:, cols] = jnp.maximum(mx[:, cols], jnp.max(s.reshape(KB // 8, 8, CB), axis=0))

    def score_body(b, carry):
        scores(b, False)
        return carry

    a2a_wait(1)
    for g in range(G):
        qr[g * T : (g + 1) * T, :] = q_all[:, g * W : (g + 1) * W]
    for d in range(1, Y):
        py_from(d).wait_recv()
    pc_copy(c).start()
    for d in range(1, Z):

        @pl.when(z - d >= 0)
        def _():
            kz_from(d).wait_recv()
            kc_copy(d).start()

    pc_copy(1 - c).wait_recv()
    units = []
    for s in range(Y * Z * 2):
        units.append(pg[s % 2, s // (2 * Z), (s // 2) % Z].astype(F32))
    per = KB // U
    for b in range(NPB):
        part = units[b * per : (b + 1) * per]
        kvb[b, 0] = jnp.concatenate([u[:U] for u in part], axis=0).astype(BF)
        kvb[b, 1] = jnp.concatenate([u[U:] for u in part], axis=0).astype(BF)

    kc_copy(0).wait_send()
    kc_from(0).wait_recv()
    scores(nb - 1, True)
    lax.fori_loop(0, NPB, score_body, 0)
    for d in range(1, Z):

        @pl.when(z - d >= 0)
        def _():
            kc_from(d).wait_recv()

    lax.fori_loop(NPB, nb - 1, score_body, 0)
    top = jnp.max(mx[...], axis=0, keepdims=True) * c2
    lx[...] = jnp.zeros_like(lx)
    o_acc[...] = jnp.zeros_like(o_acc)

    def weight_body(b, carry):
        vt = kvt[b, 1]
        for n in range(NC):
            cols = slice(n * CB, (n + 1) * CB)
            e = jnp.exp2(s_scr[b, :, cols] * c2 - top[:, cols])
            lx[:, cols] += jnp.sum(e.reshape(KB // 8, 8, CB), axis=0)
            p = e.astype(BF)
            p_scr[b, :, cols] = p
            o_acc[:, cols] += dot_nn(vt, p)
        return carry

    lax.fori_loop(0, nb, weight_body, 0)
    inv = 1.0 / jnp.sum(lx[...], axis=0, keepdims=True)

    length = len_ref[y]
    first = (2 * z + c) * T
    live_col = first + lax.broadcasted_iota(jnp.int32, (W, T), 1) < length
    live_row = first + lax.broadcasted_iota(jnp.int32, (T, W), 0) < length

    for g in range(G):
        rows = slice(g * T, (g + 1) * T)
        out_t = jnp.where(live_col, o_acc[:, rows] * inv[:, rows], 0.0)
        att_v[:, g * W : (g + 1) * W] = out_t.T.astype(BF)
        o_acc[:, rows] = out_t.astype(BF).astype(F32)
    att_out = pltpu.make_async_copy(att_v, att_ref, out_sem.at[0])
    att_out.start()

    a2a_wait(2)
    deltas = []
    for g in range(G):
        rows = slice(g * T, (g + 1) * T)
        grad = jnp.where(live_row, do_all[:, g * W : (g + 1) * W].astype(F32), 0.0)
        dor[rows, :] = grad.astype(BF)
        grad_t = grad.T
        dot_t[:, rows] = grad_t.astype(BF)
        deltas.append(jnp.sum(grad_t * o_acc[:, rows], axis=0, keepdims=True))
    delta = jnp.concatenate(deltas, axis=1)
    dq_acc[...] = jnp.zeros_like(dq_acc)

    def gx_copy(p):
        return rcopy(xs.at[p, 1 - c], xr.at[p], gx_send.at[p], gx_recv.at[p], other)

    def gz_copy(p):
        return rcopy(zs.at[p], zr.at[z - p], gz_send.at[p], gz_recv.at[z - p], at(y, p, c, h))

    def gz_from(d):
        return rcopy(zs.at[z], zr.at[d], gz_send.at[z], gz_recv.at[d], at(y, z + d, c, h))

    YB = Y // NPB

    def rc_copy(k):
        ys = pl.ds(k * YB, YB)
        return rcopy(prom_s.at[1 - c, ys], prom_r.at[ys], rc_send.at[k], rc_recv.at[k], other)

    def ry_copy(d):
        t = (y + d) % Y
        return rcopy(prom_s.at[c, t], prom_y.at[d], ry_send.at[d], ry_recv.at[d], at(t, z, c, h))

    def rz_copy(d):
        t = (z + d) % Z
        return rcopy(prom_y.at[0, t], prom_z.at[d], rz_send.at[d], rz_recv.at[d], at(y, t, c, h))

    def pass_on(p):
        gx_copy(p).wait()
        zs[p] = (xs[p, c].astype(F32) + xr[p].astype(F32)).astype(BF)
        gz_copy(p).start()

    def grad_body(b, carry):
        values = kvb[b, 1]
        kt = kvt[b, 0]
        for n in range(NC):
            cols = slice(n * CB, (n + 1) * CB)
            dp = dot_nn(values, dot_t[:, cols])
            w = p_scr[b, :, cols].astype(F32) * inv[:, cols]
            ds = (w * (dp - delta[:, cols])).astype(BF)
            dv = dot_nn(w.astype(BF), dor[cols, :])
            dk = dot_nn(ds, qr[cols, :])
            dq_acc[:, cols] += dot_nn(kt, ds)
            if n == 0:
                acc[0] = dk
                acc[1] = dv
            else:
                acc[0] += dk
                acc[1] += dv

        per_y = Z * 2

        for blk in range(NPB):

            @pl.when(b == blk)
            def _():
                for i in range(KB // U):
                    s = blk * (KB // U) + i
                    rows = slice(i * U, (i + 1) * U)
                    both = jnp.concatenate([acc[0, rows, :] * scale, acc[1, rows, :]], axis=0)
                    prom_s[s % 2, s // per_y, (s // 2) % Z] = both.astype(BF)

            @pl.when(b == blk)
            def _():
                rc_copy(blk).start()

        @pl.when(b >= NPB)
        def _():
            p = b - NPB
            for half in range(2):
                rows = slice(half * T, (half + 1) * T)
                xs[p, half, 0] = (acc[0, rows, :] * scale).astype(BF)
                xs[p, half, 1] = acc[1, rows, :].astype(BF)
            gx_copy(p).start()

        for k in range(NPB):

            @pl.when(b == k + 1)
            def _():
                rc_copy(k).wait()
                ys = slice(k * YB, (k + 1) * YB)
                prom_s[c, ys] = (prom_s[c, ys].astype(F32) + prom_r[ys].astype(F32)).astype(BF)
                for d in range(1, Y):
                    t = (y + d) % Y

                    @pl.when(t // YB == k)
                    def _():
                        ry_copy(d).start()

        @pl.when(b > NPB + 1)
        def _():
            pass_on(b - NPB - 2)

        return carry

    lax.fori_loop(0, nb, grad_body, 0)

    @pl.when(z > 0)
    def _():
        pass_on(z - 1)


    total = prom_s[c, y].astype(F32)
    for d in range(1, Y):
        ry_copy(d).wait_recv()
        total += prom_y[d].astype(F32)
    prom_y[0] = total.astype(BF)
    for d in range(1, Z):
        rz_copy(d).start()

    for g in range(G):
        rows = slice(g * T, (g + 1) * T)
        dq_v[:, g * W : (g + 1) * W] = (dq_acc[:, rows] * scale).T.astype(BF)
    dq_out = pltpu.make_async_copy(dq_v, dq_ref, out_sem.at[1])
    dq_out.start()

    gx_copy(z).wait()
    mine = xs[z, c].astype(F32) + xr[z].astype(F32)
    acc2 = acc
    acc2[0, :T] = mine[0]
    acc2[1, :T] = mine[1]
    for d in range(1, Z):

        @pl.when(z + d < Z)
        def _():
            gz_from(d).wait_recv()
            acc2[0, :T] += zr[d, 0].astype(F32)
            acc2[1, :T] += zr[d, 1].astype(F32)

    dk_v[...] = acc2[0, :T].astype(BF)
    dv_v[...] = acc2[1, :T].astype(BF)
    dk_out = pltpu.make_async_copy(dk_v, dk_ref, out_sem.at[2])
    dv_out = pltpu.make_async_copy(dv_v, dv_ref, out_sem.at[3])
    dk_out.start()
    dv_out.start()

    last = prom_y[0, z].astype(F32)
    for d in range(1, Z):
        rz_copy(d).wait_recv()
        last += prom_z[d].astype(F32)
    pdk_v[...] = last[:U]
    pdv_v[...] = last[U:]
    pdk_out = pltpu.make_async_copy(pdk_v, pdk_ref, out_sem.at[4])
    pdv_out = pltpu.make_async_copy(pdv_v, pdv_ref, out_sem.at[5])
    pdk_out.start()
    pdv_out.start()
    for copy in (att_out, dq_out, dk_out, dv_out, pdk_out, pdv_out):
        copy.wait()

    for a in range(3):
        for d in range(1, H):
            a2a_copy(a, d).wait_send()
    for d in range(1, Z):
        pz_copy(d).wait_send()
        rz_copy(d).wait_send()
    for d in range(1, Y):
        py_copy(d).wait_send()
        ry_copy(d).wait_send()
    pc_copy(c).wait_send()
    for d in range(1, Z):

        @pl.when(z + d < Z)
        def _():
            kz_copy(d).wait_send()

        @pl.when(z - d >= 0)
        def _():
            kc_copy(d).wait_send()
            gz_copy(z - d).wait_send()


def write_out(*refs):
    given, written, held, sems = refs[:6], refs[6:12], refs[12:18], refs[18]
    reads = [pltpu.make_async_copy(given[i], held[i], sems.at[0, i]) for i in range(6)]
    writes = [pltpu.make_async_copy(held[i], written[i], sems.at[1, i]) for i in range(6)]
    for copy in reads:
        copy.start()
    for i in range(6):
        reads[i].wait()
        writes[i].start()
    for copy in writes:
        copy.wait()


def solution(mesh):
    H = mesh.shape["head"]
    S = mesh.shape["seq"]

    def per_device(q, rk, rv, pk, pv, do, lengths):
        TR = q.shape[0]
        T = TR * H
        Y = lengths.shape[0]
        Z = S // Y // 2
        U = pk.shape[0]
        R = T * G
        NB = U * S // KB + Z
        dims = (H, Y, Z, TR, U)
        dma = pltpu.SemaphoreType.DMA
        vm = pltpu.VMEM
        any_spec = pl.BlockSpec(memory_space=pl.ANY)
        shapes = [
            jax.ShapeDtypeStruct((T, G * W), BF),
            jax.ShapeDtypeStruct((T, G * W), BF),
            jax.ShapeDtypeStruct((T, W), BF),
            jax.ShapeDtypeStruct((T, W), BF),
            jax.ShapeDtypeStruct((U, W), F32),
            jax.ShapeDtypeStruct((U, W), F32),
        ]
        results = pl.pallas_call(
            functools.partial(kernel, dims),
            out_shape=shapes,
            in_specs=[any_spec] * 7,
            out_specs=[any_spec] * 6,
            scratch_shapes=[
                vm((U, W), BF),
                vm((U, W), BF),
                pltpu.SMEM((Y,), jnp.int32),
                vm((2, TR, H * W), BF),
                dma((5,)),
                dma((6,)),
            ]
            + [vm(x.shape, x.dtype) for x in shapes]
            + [
                vm((T, G * W), BF),
                vm((T, G * W), BF),
                vm((NB, 2, KB, W), BF),
                vm((NB, 2, W, KB), BF),
                vm((2, Y, Z, 2 * U, W), BF),
                vm((R, W), BF),
                vm((R, W), BF),
                vm((W, R), BF),
                vm((NB, KB, R), F32),
                vm((NB, KB, R), BF),
                vm((8, R), F32),
                vm((8, R), F32),
                vm((W, R), F32),
                vm((W, R), F32),
                vm((2, KB, W), F32),
                vm((2, Y, Z, 2 * U, W), BF),
                vm((Y, Z, 2 * U, W), BF),
                vm((Y, Z, 2 * U, W), BF),
                vm((Z, 2 * U, W), BF),
                vm((Z, 2, 2, T, W), BF),
                vm((Z, 2, T, W), BF),
                vm((Z, 2, T, W), BF),
                vm((Z, 2, T, W), BF),
                dma((3, H)),
                dma((3, H)),
                dma((3,)),
                dma((Z,)),
                dma((Z,)),
                dma((Y,)),
                dma((Y,)),
                dma,
                dma,
                dma((Z,)),
                dma((Z,)),
                dma((Z,)),
                dma((Z,)),
                dma((Z,)),
                dma((Z,)),
                dma((Z,)),
                dma((Z,)),
                dma((U * S // KB,)),
                dma((U * S // KB,)),
                dma((Y,)),
                dma((Y,)),
                dma((Z,)),
                dma((Z,)),
            ],
            compiler_params=pltpu.CompilerParams(
                collective_id=0, has_side_effects=True, vmem_limit_bytes=60 * 1024 * 1024
            ),
        )(q, rk, rv, pk, pv, do, lengths)
        return pl.pallas_call(
            write_out,
            out_shape=shapes,
            in_specs=[any_spec] * 6,
            out_specs=[any_spec] * 6,
            scratch_shapes=[vm(x.shape, x.dtype) for x in shapes] + [dma((2, 6))],
            compiler_params=pltpu.CompilerParams(vmem_limit_bytes=60 * 1024 * 1024),
        )(*results)

    tok = P(("seq", "head"), None)
    par = P("seq", "head")
    return jax.shard_map(
        per_device,
        mesh=mesh,
        in_specs=(tok, tok, tok, par, par, tok, P()),
        out_specs=(par,) * 6,
        check_vma=False,
    )
```
